128 devices in a mesh: had: 8 (over z, core), blk: 16 (over x, y).
Axes of the slice: x: 4, y: 4, z: 4, core: 2. Of those that a mesh axis runs over, the one named last changes fastest.
Arguments:
- panel: bfloat16 [262144, 512], P(('had', 'blk')), may hold values from -100 to 100
- signs: int32 [262144], P(('had', 'blk')), may hold values from 0 to 1
- sample_rows: int32 [16, 2048], P('blk'), may hold values from 0 to 16383
Outputs:
- q_panel: bfloat16 [262144, 512], P(('had', 'blk'))
- r_sketch: float32 [512, 512], replicated
- r_gram: float32 [512, 512], replicated
The draws below stay inside these ranges and needn't reach their ends.
All inputs are finite; a program needn't handle non-finite values.
Results may differ from the reference program's by a relative error of at most 0.0075.
The reference program's roundings to bfloat16 on the way (of `sketch_inverse`, `whitened` and `gram_inverse`) count: a program that leaves them out, or rounds other values in their place, can miss the bound.
Values sent between devices are 32-bit elements; how exact they have to be, the bound alone decides.
No kernel may reach another device: no remote copies, remote signals or barrier semaphores. Data moves between devices by JAX's collectives and lax.ppermute only.
A program may use at most 448 MiB of HBM per device.

```python
import math
import jax
import jax.numpy as jnp
from jax import lax

K = 512
SK = 2048
LH = 32
R_DEV = 2048
BLOCK_ROWS = 16384
ROWS = 262144
N_HAD = 8
N_BLK = 16


def draw_panel(key, part):
    first_key = jax.random.fold_in(key, 11)
    column_key = jax.random.fold_in(key, 12)
    row_key = jax.random.fold_in(key, 13)
    shared_key = jax.random.fold_in(key, 15)
    pattern_key = jax.random.fold_in(key, 16)
    column_scale = jnp.exp(jax.random.uniform(column_key, (K,), jnp.float32, 0.0, math.log(10.0)))
    row_scale = jnp.exp(jax.random.uniform(row_key, (ROWS,), jnp.float32, 0.0, math.log(3.3)))
    ramp = jnp.exp(math.log(3.0) * jnp.arange(ROWS, dtype=jnp.float32) / ROWS)
    shared = jnp.clip(jax.random.normal(shared_key, (ROWS, 1), jnp.float32), -6.0, 6.0)
    pattern = jax.random.uniform(pattern_key, (1, K), jnp.float32, -1.5, 1.5)
    base = jnp.clip(jax.random.normal(first_key, (ROWS, K), jnp.float32), -6.0, 6.0)
    base = base + 3.5 * shared * pattern
    values = 0.15 * base * column_scale[None, :] * (row_scale * ramp)[:, None]
    values = jnp.clip(values, -100.0, 100.0)
    return values.astype(jnp.bfloat16)


def touch_ends(array, own_key, smallest, top_value):
    extent = array.shape
    place = [jax.random.randint(jax.random.fold_in(own_key, axis), (), 0, extent[axis]) for axis in range(len(extent))]
    array = array.at[tuple(place)].set(smallest)
    longest = extent.index(max(extent))
    place[longest] = (place[longest] + 1) % extent[longest]
    return array.at[tuple(place)].set(top_value)


def setup_inputs(seed: int = 0) -> dict:
    keys = jax.random.split(jax.random.key(seed), 4)
    return {
        "panel": draw_panel(jax.random.fold_in(keys[3], 71), 0),
        "signs": touch_ends(jax.random.randint(keys[1], (ROWS,), 0, 2), jax.random.fold_in(keys[1], 1), 0, 1).astype(jnp.int32),
        "sample_rows": touch_ends(jax.random.randint(keys[2], (N_BLK, SK), 0, BLOCK_ROWS), jax.random.fold_in(keys[2], 1), 0, BLOCK_ROWS - 1).astype(jnp.int32),
    }


def bit_parity(value):
    counted = jnp.zeros_like(value)
    for shift_count in range(16):
        counted = counted + jnp.bitwise_and(jnp.right_shift(value, shift_count), 1)
    return counted % 2

def hadamard(order):
    first = lax.broadcasted_iota(jnp.int32, (order, order), 0)
    second = lax.broadcasted_iota(jnp.int32, (order, order), 1)
    parity = bit_parity(jnp.bitwise_and(first, second))
    return (1 - 2 * parity).astype(jnp.float32)

def upper_factor(matrix):
    return jnp.linalg.cholesky(matrix).T

def lower_inverse(lower):
    order = lower.shape[0]
    inverse = (1.0 / jnp.diagonal(lower)).reshape(order, 1, 1)
    width = 1
    while width < order:
        count = order // (2 * width)
        tiles = lower.reshape(count, 2 * width, count, 2 * width)
        diag_tiles = jnp.moveaxis(jnp.diagonal(tiles, axis1=0, axis2=2), -1, 0)
        corner = diag_tiles[:, width:, :width]
        first_inv = inverse[0::2]
        second_inv = inverse[1::2]
        partial_value = jnp.einsum('ajk,akl->ajl', corner, first_inv, precision=lax.Precision.HIGHEST)
        lower_left = -jnp.einsum('aij,ajl->ail', second_inv, partial_value, precision=lax.Precision.HIGHEST)
        zero_tile = jnp.zeros_like(corner)
        top_half = jnp.concatenate([first_inv, zero_tile], axis=2)
        bottom_half = jnp.concatenate([lower_left, second_inv], axis=2)
        inverse = jnp.concatenate([top_half, bottom_half], axis=1)
        width = width * 2
    return inverse[0]

def inverse_upper(factor):
    return lower_inverse(factor.T).T

def reference(panel, signs, sample_rows):
    groups = R_DEV // LH
    flips = (1 - 2 * signs).astype(jnp.float32)
    blocks = panel.reshape(N_HAD, N_BLK, groups, LH, K)
    flip_blocks = flips.reshape(N_HAD, N_BLK, groups, LH)
    outer = hadamard(N_HAD)
    inner = hadamard(LH)
    factor = 1.0 / math.sqrt(N_HAD * LH * SK * N_BLK)

    def add_block(which, summed):
        member = lax.dynamic_index_in_dim(blocks, which, 1, keepdims=False).astype(jnp.float32)
        member_flips = lax.dynamic_index_in_dim(flip_blocks, which, 1, keepdims=False)
        signed = member * member_flips[..., None]
        mixed = jnp.einsum('ml,hglk->hgmk', inner, signed, precision=lax.Precision.HIGHEST)
        mixed = jnp.einsum('ph,hgmk->pgmk', outer, mixed, precision=lax.Precision.HIGHEST)
        mixed = mixed.reshape(N_HAD * R_DEV, K)
        picks = lax.dynamic_index_in_dim(sample_rows, which, 0, keepdims=False)
        return summed + jnp.take(mixed, picks, axis=0)
    summed = lax.fori_loop(0, N_BLK, add_block, jnp.zeros((SK, K), jnp.float32))
    sketch = summed * factor
    sketch_gram = jnp.dot(sketch.T.astype(jnp.float32), sketch.astype(jnp.float32), precision=lax.Precision.HIGHEST, preferred_element_type=jnp.float32)
    r_sketch = upper_factor(sketch_gram)
    sketch_inverse = inverse_upper(r_sketch).astype(jnp.bfloat16)
    whitened = jnp.dot(panel.astype(jnp.float32), sketch_inverse.astype(jnp.float32), preferred_element_type=jnp.float32).astype(jnp.bfloat16)
    gram = jnp.dot(whitened.T.astype(jnp.float32), whitened.astype(jnp.float32), preferred_element_type=jnp.float32) / ROWS
    r_gram = upper_factor(gram)
    gram_inverse = inverse_upper(r_gram).astype(jnp.bfloat16)
    q_panel = jnp.dot(whitened.astype(jnp.float32), gram_inverse.astype(jnp.float32), preferred_element_type=jnp.float32).astype(jnp.bfloat16)
    return (q_panel, r_sketch, r_gram)
```

```python
import functools

import jax
import jax.numpy as jnp
from jax import lax
from jax.experimental import pallas as pl
from jax.experimental.pallas import tpu as pltpu
from jax.sharding import Mesh, PartitionSpec as P

LH = 32
NB = 64
GB = 128
AXES = ("z", "c", "x", "y")
CHIPS = ("z", "x", "y")
HIGHEST = lax.Precision.HIGHEST
VMEM = pl.BlockSpec(memory_space=pltpu.VMEM)
PARAMS = pltpu.CompilerParams(vmem_limit_bytes=48 * 1024 * 1024)


def dot(first, second, first_dim=1, second_dim=0, precision=None):
    return lax.dot_general(
        first,
        second,
        (((first_dim,), (second_dim,)), ((), ())),
        precision=precision,
        preferred_element_type=jnp.float32,
    )


def upper_blocks(columns):
    count = columns // GB
    return [(i, j) for i in range(count) for j in range(i, count)]


def sketch_kernel(codes_ref, signs_ref, panel_ref, out_ref):
    rows = panel_ref.shape[0]
    lane = lax.broadcasted_iota(jnp.int32, (128, 128), 1)
    inner_lane = jnp.bitwise_and(lane, LH - 1)
    group_lane = lane // LH
    flips = (1 - 2 * signs_ref[...]).astype(jnp.float32)
    for chunk in range(codes_ref.shape[1] // 256):
        strips = []
        for part in range(2):
            start = chunk * 256 + part * 128
            code = jnp.broadcast_to(codes_ref[:, start : start + 128], (128, 128)).T
            bits = jnp.bitwise_and(jnp.bitwise_and(code, LH - 1), inner_lane)
            bits = jnp.bitwise_xor(bits, jnp.right_shift(bits, 4))
            bits = jnp.bitwise_xor(bits, jnp.right_shift(bits, 2))
            bits = jnp.bitwise_xor(bits, jnp.right_shift(bits, 1))
            bits = jnp.bitwise_xor(bits, jnp.right_shift(code, 16))
            values = (1 - 2 * jnp.bitwise_and(bits, 1)).astype(jnp.float32)
            group = jnp.bitwise_and(jnp.right_shift(code, 5), 63) - group_lane
            strips.append((values, group))
        tiles = []
        for tile in range(rows // 128):
            flip = flips[:, tile * 128 : tile * 128 + 128]
            tiles.append(
                jnp.concatenate(
                    [jnp.where(group == 4 * tile, values * flip, 0.0).astype(jnp.bfloat16)
                     for values, group in strips],
                    axis=0,
                )
            )
        chosen = jnp.concatenate(tiles, axis=1)
        out_ref[chunk * 256 : chunk * 256 + 256, :] = dot(chosen, panel_ref[...])


def sketch_rows(codes, signs, panel):
    return pl.pallas_call(
        sketch_kernel,
        out_shape=jax.ShapeDtypeStruct((codes.shape[1], panel.shape[1]), jnp.float32),
        in_specs=[VMEM] * 3,
        out_specs=VMEM,
        compiler_params=PARAMS,
        name="sketch_rows",
    )(codes, signs, panel)


def pack_gram(matrix, out_ref, precision):
    columns = matrix.shape[1]
    place = 0
    for i in range(columns // GB):
        strip = dot(matrix[:, i * GB : i * GB + GB], matrix[:, i * GB :], 0, 0, precision)
        for j in range(columns // GB - i):
            out_ref[place * GB : place * GB + GB, :] = strip[:, j * GB : j * GB + GB]
            place += 1


def sketch_gram_kernel(parts_ref, out_ref):
    total = jnp.sum(parts_ref[...], axis=0)
    pack_gram(total, out_ref, HIGHEST)


def sketch_gram(parts):
    columns = parts.shape[2]
    return pl.pallas_call(
        sketch_gram_kernel,
        out_shape=jax.ShapeDtypeStruct((len(upper_blocks(columns)) * GB, GB), jnp.float32),
        in_specs=[VMEM],
        out_specs=VMEM,
        compiler_params=PARAMS,
        name="sketch_gram",
    )(parts)


def whiten_kernel(panel_ref, inverse_ref, white_ref, out_ref):
    rows = panel_ref.shape[0]
    for start in range(0, rows, 256):
        white_ref[start : start + 256, :] = dot(
            panel_ref[start : start + 256, :], inverse_ref[...], 1, 1
        ).astype(jnp.bfloat16)
    pack_gram(white_ref[...], out_ref, None)


def whiten(panel, inverse):
    columns = panel.shape[1]
    return pl.pallas_call(
        whiten_kernel,
        out_shape=(
            jax.ShapeDtypeStruct(panel.shape, jnp.bfloat16),
            jax.ShapeDtypeStruct((len(upper_blocks(columns)) * GB, GB), jnp.float32),
        ),
        in_specs=[VMEM] * 2,
        out_specs=(VMEM, VMEM),
        compiler_params=PARAMS,
        name="whiten",
    )(panel, inverse)


def factor_block(block):
    row = lax.broadcasted_iota(jnp.int32, (NB, NB), 0)
    column = lax.broadcasted_iota(jnp.int32, (NB, NB), 1)
    both = jnp.concatenate([block, (row == column).astype(jnp.float32)], axis=1)
    count = NB // 8
    work = [both[8 * u : 8 * u + 8, :] for u in range(count)]
    sub = lax.broadcasted_iota(jnp.int32, (8, 128), 0)
    done = [None] * count
    for j in range(NB):
        t, k = divmod(j, 8)
        lanes = {u: jnp.broadcast_to(work[u][:, j : j + 1], (8, 128)) for u in range(t, count)}
        pivot_row = jnp.broadcast_to(work[t][k : k + 1, :], (8, 128))
        pivot = jnp.broadcast_to(lanes[t][k : k + 1, :], (8, 128))
        scaled = pivot_row * (1.0 / pivot)
        final = pivot_row * lax.rsqrt(pivot)
        done[t] = final if k == 0 else jnp.where(sub == k, final, done[t])
        if k < 7:
            work[t] = jnp.where(sub > k, work[t] - lanes[t] * scaled, work[t])
        for u in range(t + 1, count):
            work[u] = work[u] - lanes[u] * scaled
    return jnp.concatenate(done, axis=0)


def factor_kernel(scale, packed_ref, factor_ref, inverse_ref, work):
    order = work.shape[0]
    for place, (i, j) in enumerate(upper_blocks(order)):
        block = packed_ref[place * GB : place * GB + GB, :] * scale
        work[i * GB : i * GB + GB, j * GB : j * GB + GB] = block
        if i != j:
            work[j * GB : j * GB + GB, i * GB : i * GB + GB] = block.T
    row = lax.broadcasted_iota(jnp.int32, (NB, NB), 0)
    column = lax.broadcasted_iota(jnp.int32, (NB, NB), 1)
    wide = lax.broadcasted_iota(jnp.int32, (NB, order), 1)
    for end in range(NB, order + 1, NB):
        own = slice(end - NB, end)
        rest = slice(end, order)
        both = factor_block(work[own, own])
        diagonal = jnp.where(row <= column, both[:, :NB], 0.0)
        inverse = both[:, NB:]
        if end < order:
            left = dot(work[rest, own], inverse, 1, 1, HIGHEST)
        work[own, own] = (row == column).astype(jnp.float32)
        strip = dot(inverse, work[own, :], 1, 0, HIGHEST)
        inverse_ref[own, :] = jnp.where(wide < end, strip, 0.0).astype(jnp.bfloat16)
        factor_ref[own, :] = jnp.where(wide >= end, strip, 0.0)
        factor_ref[own, own] = diagonal
        if end < order:
            work[rest, own] = jnp.zeros((order - end, NB), jnp.float32)
            work[rest, :] = work[rest, :] - dot(left, strip, 1, 0, HIGHEST)


def factor(packed, order, scale):
    return pl.pallas_call(
        functools.partial(factor_kernel, scale),
        out_shape=(
            jax.ShapeDtypeStruct((order, order), jnp.float32),
            jax.ShapeDtypeStruct((order, order), jnp.bfloat16),
        ),
        in_specs=[VMEM],
        out_specs=(VMEM, VMEM),
        scratch_shapes=[pltpu.VMEM((order, order), jnp.float32)],
        compiler_params=PARAMS,
        name="factor",
    )(packed)


def sum_all(packed):
    count = lax.axis_size(AXES)
    chunk = packed.shape[0] // count
    parts = packed.reshape(count, chunk // 2, 2, GB)
    parts = lax.all_to_all(parts, AXES, 0, 0, tiled=True)
    total = jnp.sum(parts, axis=0, keepdims=True)
    parts = jnp.broadcast_to(total, parts.shape)
    parts = lax.all_to_all(parts, AXES, 0, 0, tiled=True)
    return parts.reshape(packed.shape)


def parity(value):
    for shift in (8, 4, 2, 1):
        value = jnp.bitwise_xor(value, jnp.right_shift(value, shift))
    return jnp.bitwise_and(value, 1)


def on_device(panel, signs, sample_rows):
    core = lax.axis_index("c")
    n_had = lax.axis_size("z") * lax.axis_size("c")
    n_blk = lax.axis_size("x") * lax.axis_size("y")
    my_group = lax.axis_index(("z", "c"))
    rows_dev, columns = panel.shape
    sketch_count = sample_rows.shape[1]
    half = sketch_count // 2
    owners = sample_rows // rows_dev
    offsets = sample_rows % rows_dev
    codes = offsets + 65536 * parity(jnp.bitwise_and(owners, my_group))
    signs = signs.reshape(1, rows_dev)
    sent = lax.dynamic_slice_in_dim(codes, (1 - core) * half, half, 1)
    kept = lax.dynamic_slice_in_dim(codes, core * half, half, 1)
    other = lax.ppermute(sketch_rows(sent, signs, panel), "c", [(0, 1), (1, 0)])
    mine = sketch_rows(kept, signs, panel) + other
    chips = lax.axis_size(CHIPS)
    mine = mine.reshape(chips, half // chips, columns)
    parts = lax.all_to_all(mine, CHIPS, 0, 0, tiled=True)
    packed = sum_all(sketch_gram(parts))
    r_sketch, sketch_inverse = factor(
        packed, columns, 1.0 / (n_had * LH * sketch_count * n_blk)
    )
    whitened, packed = whiten(panel, sketch_inverse)
    packed = sum_all(packed)
    r_gram, gram_inverse = factor(packed, columns, 1.0 / (rows_dev * n_had * n_blk))
    q_panel = dot(whitened, gram_inverse, 1, 1).astype(jnp.bfloat16)
    return (q_panel, r_sketch, r_gram)


def solution(mesh):
    devices = mesh.devices.reshape(4, 2, 4, 4)
    split = Mesh(devices, AXES)
    placed = (P(AXES, None), P(AXES), P(("x", "y"), None))
    return jax.shard_map(
        on_device,
        mesh=split,
        in_specs=placed,
        out_specs=(P(AXES, None), P(), P()),
        check_vma=False,
    )
```

```python
import functools

import jax
import jax.numpy as jnp
from jax import lax
from jax.experimental import pallas as pl
from jax.experimental.pallas import tpu as pltpu
from jax.sharding import Mesh, PartitionSpec as P

LH = 32
NB = 64
GB = 128
AXES = ("z", "c", "x", "y")
CHIPS = ("z", "x", "y")
HIGHEST = lax.Precision.HIGHEST
VMEM = pl.BlockSpec(memory_space=pltpu.VMEM)
PARAMS = pltpu.CompilerParams(vmem_limit_bytes=48 * 1024 * 1024)


def dot(first, second, first_dim=1, second_dim=0, precision=None):
    return lax.dot_general(
        first,
        second,
        (((first_dim,), (second_dim,)), ((), ())),
        precision=precision,
        preferred_element_type=jnp.float32,
    )


def upper_blocks(columns):
    count = columns // GB
    return [(i, j) for i in range(count) for j in range(i, count)]


def sketch_kernel(codes_ref, signs_ref, panel_ref, out_ref):
    rows = panel_ref.shape[0]
    lane = lax.broadcasted_iota(jnp.int32, (128, 128), 1)
    inner_lane = jnp.bitwise_and(lane, LH - 1)
    group_lane = lane // LH
    flips = (1 - 2 * signs_ref[...]).astype(jnp.float32)
    for chunk in range(codes_ref.shape[1] // 256):
        strips = []
        for part in range(2):
            start = chunk * 256 + part * 128
            code = jnp.broadcast_to(codes_ref[:, start : start + 128], (128, 128)).T
            bits = jnp.bitwise_and(jnp.bitwise_and(code, LH - 1), inner_lane)
            bits = jnp.bitwise_xor(bits, jnp.right_shift(bits, 4))
            bits = jnp.bitwise_xor(bits, jnp.right_shift(bits, 2))
            bits = jnp.bitwise_xor(bits, jnp.right_shift(bits, 1))
            bits = jnp.bitwise_xor(bits, jnp.right_shift(code, 16))
            values = (1 - 2 * jnp.bitwise_and(bits, 1)).astype(jnp.float32)
            group = jnp.bitwise_and(jnp.right_shift(code, 5), 63) - group_lane
            strips.append((values, group))
        tiles = []
        for tile in range(rows // 128):
            flip = flips[:, tile * 128 : tile * 128 + 128]
            tiles.append(
                jnp.concatenate(
                    [jnp.where(group == 4 * tile, values * flip, 0.0).astype(jnp.bfloat16)
                     for values, group in strips],
                    axis=0,
                )
            )
        chosen = jnp.concatenate(tiles, axis=1)
        out_ref[chunk * 256 : chunk * 256 + 256, :] = dot(chosen, panel_ref[...])


def sketch_rows(codes, signs, panel):
    return pl.pallas_call(
        sketch_kernel,
        out_shape=jax.ShapeDtypeStruct((codes.shape[1], panel.shape[1]), jnp.float32),
        in_specs=[VMEM] * 3,
        out_specs=VMEM,
        compiler_params=PARAMS,
        name="sketch_rows",
    )(codes, signs, panel)


def pack_gram(matrix, out_ref, precision):
    columns = matrix.shape[1]
    place = 0
    for i in range(columns // GB):
        strip = dot(matrix[:, i * GB : i * GB + GB], matrix[:, i * GB :], 0, 0, precision)
        for j in range(columns // GB - i):
            out_ref[place * GB : place * GB + GB, :] = strip[:, j * GB : j * GB + GB]
            place += 1


def sketch_gram_kernel(parts_ref, out_ref):
    total = jnp.sum(parts_ref[...], axis=0)
    pack_gram(total, out_ref, HIGHEST)


def sketch_gram(parts):
    columns = parts.shape[2]
    return pl.pallas_call(
        sketch_gram_kernel,
        out_shape=jax.ShapeDtypeStruct((len(upper_blocks(columns)) * GB, GB), jnp.float32),
        in_specs=[VMEM],
        out_specs=VMEM,
        compiler_params=PARAMS,
        name="sketch_gram",
    )(parts)


def whiten_kernel(panel_ref, inverse_ref, white_ref, out_ref):
    rows = panel_ref.shape[0]
    for start in range(0, rows, 256):
        white_ref[start : start + 256, :] = dot(
            panel_ref[start : start + 256, :], inverse_ref[...], 1, 1
        ).astype(jnp.bfloat16)
    pack_gram(white_ref[...], out_ref, None)


def whiten(panel, inverse):
    columns = panel.shape[1]
    return pl.pallas_call(
        whiten_kernel,
        out_shape=(
            jax.ShapeDtypeStruct(panel.shape, jnp.bfloat16),
            jax.ShapeDtypeStruct((len(upper_blocks(columns)) * GB, GB), jnp.float32),
        ),
        in_specs=[VMEM] * 2,
        out_specs=(VMEM, VMEM),
        compiler_params=PARAMS,
        name="whiten",
    )(panel, inverse)


def spread_row(tile, k):
    return jnp.broadcast_to(tile[k : k + 1, :], tile.shape)


def factor_block(block):
    row = lax.broadcasted_iota(jnp.int32, (NB, NB), 0)
    column = lax.broadcasted_iota(jnp.int32, (NB, NB), 1)
    both = jnp.concatenate([block, (row == column).astype(jnp.float32)], axis=1)
    count = NB // 8
    work = [both[8 * u : 8 * u + 8, :] for u in range(count)]
    sub = lax.broadcasted_iota(jnp.int32, (8, 128), 0)
    done = []
    for t in range(count):
        first = 8 * t
        lanes = {
            u: [jnp.broadcast_to(work[u][:, first + c : first + c + 1], (8, 128)) for c in range(8)]
            for u in range(t, count)
        }
        pivots = None
        for k in range(8):
            pivot = spread_row(lanes[t][k], k)
            pivots = pivot if k == 0 else jnp.where(sub == k, pivot, pivots)
            inverse = 1.0 / pivot
            across = {c: spread_row(lanes[t][c], k) for c in range(k + 1, 8)}
            pivot_row = spread_row(work[t], k)
            for u in range(t, count):
                if u == t and k == 7:
                    continue
                ratio = lanes[u][k] * inverse
                if u == t:
                    ratio = jnp.where(sub > k, ratio, 0.0)
                for c in range(k + 1, 8):
                    lanes[u][c] = lanes[u][c] - ratio * across[c]
                work[u] = work[u] - ratio * pivot_row
        done.append(work[t] * lax.rsqrt(pivots))
    return jnp.concatenate(done, axis=0)


def factor_kernel(scale, packed_ref, factor_ref, inverse_ref, work):
    order = work.shape[0]
    for place, (i, j) in enumerate(upper_blocks(order)):
        block = packed_ref[place * GB : place * GB + GB, :] * scale
        work[i * GB : i * GB + GB, j * GB : j * GB + GB] = block
        if i != j:
            work[j * GB : j * GB + GB, i * GB : i * GB + GB] = block.T
    row = lax.broadcasted_iota(jnp.int32, (NB, NB), 0)
    column = lax.broadcasted_iota(jnp.int32, (NB, NB), 1)
    wide = lax.broadcasted_iota(jnp.int32, (NB, order), 1)
    for end in range(NB, order + 1, NB):
        own = slice(end - NB, end)
        rest = slice(end, order)
        both = factor_block(work[own, own])
        diagonal = jnp.where(row <= column, both[:, :NB], 0.0)
        inverse = both[:, NB:]
        if end < order:
            left = dot(work[rest, own], inverse, 1, 1, HIGHEST)
        work[own, own] = (row == column).astype(jnp.float32)
        strip = dot(inverse, work[own, :], 1, 0, HIGHEST)
        inverse_ref[own, :] = jnp.where(wide < end, strip, 0.0).astype(jnp.bfloat16)
        factor_ref[own, :] = jnp.where(wide >= end, strip, 0.0)
        factor_ref[own, own] = diagonal
        if end < order:
            work[rest, own] = jnp.zeros((order - end, NB), jnp.float32)
            work[rest, :] = work[rest, :] - dot(left, strip, 1, 0, HIGHEST)


def factor(packed, order, scale):
    return pl.pallas_call(
        functools.partial(factor_kernel, scale),
        out_shape=(
            jax.ShapeDtypeStruct((order, order), jnp.float32),
            jax.ShapeDtypeStruct((order, order), jnp.bfloat16),
        ),
        in_specs=[VMEM],
        out_specs=(VMEM, VMEM),
        scratch_shapes=[pltpu.VMEM((order, order), jnp.float32)],
        compiler_params=PARAMS,
        name="factor",
    )(packed)


def sum_all(packed):
    count = lax.axis_size(AXES)
    chunk = packed.shape[0] // count
    parts = packed.reshape(count, chunk // 2, 2, GB)
    parts = lax.all_to_all(parts, AXES, 0, 0, tiled=True)
    total = jnp.sum(parts, axis=0, keepdims=True)
    parts = jnp.broadcast_to(total, parts.shape)
    parts = lax.all_to_all(parts, AXES, 0, 0, tiled=True)
    return parts.reshape(packed.shape)


def parity(value):
    for shift in (8, 4, 2, 1):
        value = jnp.bitwise_xor(value, jnp.right_shift(value, shift))
    return jnp.bitwise_and(value, 1)


def on_device(panel, signs, sample_rows):
    core = lax.axis_index("c")
    n_had = lax.axis_size("z") * lax.axis_size("c")
    n_blk = lax.axis_size("x") * lax.axis_size("y")
    my_group = lax.axis_index(("z", "c"))
    rows_dev, columns = panel.shape
    sketch_count = sample_rows.shape[1]
    half = sketch_count // 2
    owners = sample_rows // rows_dev
    offsets = sample_rows % rows_dev
    codes = offsets + 65536 * parity(jnp.bitwise_and(owners, my_group))
    signs = signs.reshape(1, rows_dev)
    sent = lax.dynamic_slice_in_dim(codes, (1 - core) * half, half, 1)
    kept = lax.dynamic_slice_in_dim(codes, core * half, half, 1)
    other = lax.ppermute(sketch_rows(sent, signs, panel), "c", [(0, 1), (1, 0)])
    mine = sketch_rows(kept, signs, panel) + other
    chips = lax.axis_size(CHIPS)
    mine = mine.reshape(chips, half // chips, columns)
    parts = lax.all_to_all(mine, CHIPS, 0, 0, tiled=True)
    packed = sum_all(sketch_gram(parts))
    r_sketch, sketch_inverse = factor(
        packed, columns, 1.0 / (n_had * LH * sketch_count * n_blk)
    )
    whitened, packed = whiten(panel, sketch_inverse)
    packed = sum_all(packed)
    r_gram, gram_inverse = factor(packed, columns, 1.0 / (rows_dev * n_had * n_blk))
    q_panel = dot(whitened, gram_inverse, 1, 1).astype(jnp.bfloat16)
    return (q_panel, r_sketch, r_gram)


def solution(mesh):
    devices = mesh.devices.reshape(4, 2, 4, 4)
    split = Mesh(devices, AXES)
    placed = (P(AXES, None), P(AXES), P(("x", "y"), None))
    return jax.shard_map(
        on_device,
        mesh=split,
        in_specs=placed,
        out_specs=(P(AXES, None), P(), P()),
        check_vma=False,
    )
```

```python
import functools

import jax
import jax.numpy as jnp
from jax import lax
from jax.experimental import pallas as pl
from jax.experimental.pallas import tpu as pltpu
from jax.sharding import Mesh, PartitionSpec as P

LH = 32
NB = 64
GB = 128
AXES = ("z", "c", "x", "y")
CHIPS = ("z", "x", "y")
HIGHEST = lax.Precision.HIGHEST
VMEM = pl.BlockSpec(memory_space=pltpu.VMEM)
PARAMS = pltpu.CompilerParams(vmem_limit_bytes=48 * 1024 * 1024)


def dot(first, second, first_dim=1, second_dim=0, precision=None):
    return lax.dot_general(
        first,
        second,
        (((first_dim,), (second_dim,)), ((), ())),
        precision=precision,
        preferred_element_type=jnp.float32,
    )


def upper_blocks(columns):
    count = columns // GB
    return [(i, j) for i in range(count) for j in range(i, count)]


def parity(value):
    for shift in (4, 2, 1):
        value = jnp.bitwise_xor(value, jnp.right_shift(value, shift))
    return jnp.bitwise_and(value, 1)


def sketch_kernel(own_half, picks_ref, signs_ref, panel_ref, out_ref):
    rows = panel_ref.shape[0]
    group_mine = lax.axis_index("z") * lax.axis_size("c") + lax.axis_index("c")
    half = lax.axis_index("c") if own_half else 1 - lax.axis_index("c")
    lane = lax.broadcasted_iota(jnp.int32, (128, 128), 1)
    inner_lane = jnp.bitwise_and(lane, LH - 1)
    group_lane = lane // LH
    flips = (1 - 2 * signs_ref[...]).astype(jnp.float32)
    for chunk in range(out_ref.shape[0] // 256):
        strips = []
        for part in range(2):
            start = pl.multiple_of(half * out_ref.shape[0] + chunk * 256 + part * 128, 128)
            picks = jnp.broadcast_to(picks_ref[:, pl.ds(start, 128)], (128, 128)).T
            owners = jnp.right_shift(picks, rows.bit_length() - 1)
            bits = jnp.bitwise_and(jnp.bitwise_and(picks, LH - 1), inner_lane)
            bits = parity(jnp.bitwise_xor(bits, parity(jnp.bitwise_and(owners, group_mine))))
            values = (1 - 2 * bits).astype(jnp.float32)
            group = jnp.right_shift(jnp.bitwise_and(picks, rows - 1), 5) - group_lane
            strips.append((values, group))
        tiles = []
        for tile in range(rows // 128):
            flip = flips[:, tile * 128 : tile * 128 + 128]
            tiles.append(
                jnp.concatenate(
                    [jnp.where(group == 4 * tile, values * flip, 0.0).astype(jnp.bfloat16)
                     for values, group in strips],
                    axis=0,
                )
            )
        chosen = jnp.concatenate(tiles, axis=1)
        out_ref[chunk * 256 : chunk * 256 + 256, :] = dot(chosen, panel_ref[...])


def sketch_rows(own_half, picks, signs, panel):
    return pl.pallas_call(
        functools.partial(sketch_kernel, own_half),
        out_shape=jax.ShapeDtypeStruct((picks.shape[1] // 2, panel.shape[1]), jnp.float32),
        in_specs=[VMEM] * 3,
        out_specs=VMEM,
        compiler_params=PARAMS,
        name="sketch_own" if own_half else "sketch_sent",
    )(picks, signs, panel)


def pack_gram(matrix, kept_ref, sent_ref, precision):
    columns = matrix.shape[1]
    blocks = []
    for i in range(columns // GB):
        strip = dot(matrix[:, i * GB : i * GB + GB], matrix[:, i * GB :], 0, 0, precision)
        blocks += [strip[:, j * GB : j * GB + GB] for j in range(columns // GB - i)]
    first = lax.axis_index("c") == 0
    half = len(blocks) // 2
    for place in range(half):
        own = slice(place * GB, place * GB + GB)
        kept_ref[own, :] = jnp.where(first, blocks[place], blocks[place + half])
        sent_ref[own, :] = jnp.where(first, blocks[place + half], blocks[place])


def half_shape(columns):
    return jax.ShapeDtypeStruct((len(upper_blocks(columns)) // 2 * GB, GB), jnp.float32)


def sketch_gram_kernel(parts_ref, kept_ref, sent_ref):
    pack_gram(jnp.sum(parts_ref[...], axis=0), kept_ref, sent_ref, HIGHEST)


def sketch_gram(parts):
    columns = parts.shape[2]
    return pl.pallas_call(
        sketch_gram_kernel,
        out_shape=(half_shape(columns),) * 2,
        in_specs=[VMEM],
        out_specs=(VMEM, VMEM),
        compiler_params=PARAMS,
        name="sketch_gram",
    )(parts)


def times_inverse(rows_ref, inverse, buffer, out_ref, sems):
    rows, columns = rows_ref.shape
    half = columns // 2
    copies = []
    for place, start in enumerate(range(0, rows, 512)):
        own = pl.ds(start, 512)
        buffer[own, :half] = dot(
            rows_ref[own, :half], inverse[:half, :half], 1, 1
        ).astype(jnp.bfloat16)
        buffer[own, half:] = dot(rows_ref[own, :], inverse[half:, :], 1, 1).astype(jnp.bfloat16)
        copies.append(pltpu.make_async_copy(buffer.at[own, :], out_ref.at[own, :], sems.at[place]))
        copies[-1].start()
    return copies


def spread_row(tile, k):
    return jnp.broadcast_to(tile[k : k + 1, :], tile.shape)


def factor_block(block):
    row = lax.broadcasted_iota(jnp.int32, (NB, NB), 0)
    column = lax.broadcasted_iota(jnp.int32, (NB, NB), 1)
    both = jnp.concatenate([block, (row == column).astype(jnp.float32)], axis=1)
    count = NB // 8
    work = [both[8 * u : 8 * u + 8, :] for u in range(count)]
    sub = lax.broadcasted_iota(jnp.int32, (8, 128), 0)
    done = []
    for t in range(count):
        first = 8 * t
        lanes = {
            u: [jnp.broadcast_to(work[u][:, first + c : first + c + 1], (8, 128)) for c in range(8)]
            for u in range(t, count)
        }
        pivots = None
        for k in range(8):
            pivot = spread_row(lanes[t][k], k)
            pivots = pivot if k == 0 else jnp.where(sub == k, pivot, pivots)
            inverse = 1.0 / pivot
            across = {c: spread_row(lanes[t][c], k) for c in range(k + 1, 8)}
            pivot_row = spread_row(work[t], k)
            for u in range(t, count):
                if u == t and k == 7:
                    continue
                ratio = lanes[u][k] * inverse
                if u == t:
                    ratio = jnp.where(sub > k, ratio, 0.0)
                for c in range(k + 1, 8):
                    lanes[u][c] = lanes[u][c] - ratio * across[c]
                work[u] = work[u] - ratio * pivot_row
        done.append(work[t] * lax.rsqrt(pivots))
    return jnp.concatenate(done, axis=0)


def split(value):
    first = value.astype(jnp.bfloat16)
    left = value - first.astype(jnp.float32)
    second = left.astype(jnp.bfloat16)
    third = (left - second.astype(jnp.float32)).astype(jnp.bfloat16)
    return first, second, third


def left_terms(value, axis):
    first, second, third = split(value)
    return jnp.concatenate([first, first, second, second, first, third], axis=axis)


def right_terms(value, axis):
    first, second, third = split(value)
    return jnp.concatenate([first, second, first, second, third, first], axis=axis)


def factor_into(scale, own_ref, other_ref, factor_ref, inverse_ref, work):
    order = work.shape[0]
    first = lax.axis_index("c") == 0
    blocks = upper_blocks(order)
    half = len(blocks) // 2
    for place in range(half):
        rows = slice(place * GB, place * GB + GB)
        own, other = own_ref[rows, :] * scale, other_ref[rows, :] * scale
        for which, block in (
            (place, jnp.where(first, own, other)),
            (place + half, jnp.where(first, other, own)),
        ):
            i, j = blocks[which]
            work[i * GB : i * GB + GB, j * GB : j * GB + GB] = block
            if i != j:
                work[j * GB : j * GB + GB, i * GB : i * GB + GB] = block.T
    row = lax.broadcasted_iota(jnp.int32, (NB, NB), 0)
    column = lax.broadcasted_iota(jnp.int32, (NB, NB), 1)
    wide = lax.broadcasted_iota(jnp.int32, (NB, order), 1)
    for end in range(NB, order + 1, NB):
        own = slice(end - NB, end)
        rest = slice(end, order)
        both = factor_block(work[own, own])
        diagonal = jnp.where(row <= column, both[:, :NB], 0.0)
        inverse = left_terms(both[:, NB:], 1)
        if end < order:
            left = dot(right_terms(work[rest, own], 1), inverse, 1, 1)
        work[own, own] = (row == column).astype(jnp.float32)
        strip = dot(inverse, right_terms(work[own, :], 0))
        inverse_ref[own, :] = jnp.where(wide < end, strip, 0.0).astype(jnp.bfloat16)
        factor_ref[own, :] = jnp.where(wide >= end, strip, 0.0)
        factor_ref[own, own] = diagonal
        if end < order:
            work[rest, own] = jnp.zeros((order - end, NB), jnp.float32)
            work[rest, :] = work[rest, :] - dot(left_terms(left, 1), right_terms(strip, 0))


def whiten_kernel(
    scale, own_ref, other_ref, panel_ref, factor_ref, white_ref, kept_ref, sent_ref,
    work, inverse, buffer, sems,
):
    factor_into(scale, own_ref, other_ref, factor_ref, inverse, work)
    copies = times_inverse(panel_ref, inverse, buffer, white_ref, sems)
    pack_gram(buffer[...], kept_ref, sent_ref, None)
    for copy in copies:
        copy.wait()


def finish_kernel(
    scale, own_ref, other_ref, white_ref, factor_ref, out_ref, work, inverse, buffer, sems
):
    factor_into(scale, own_ref, other_ref, factor_ref, inverse, work)
    for copy in times_inverse(white_ref, inverse, buffer, out_ref, sems):
        copy.wait()


def factor_and_apply(kernel, name, extra, scale, own, other, matrix):
    rows, order = matrix.shape
    return pl.pallas_call(
        functools.partial(kernel, scale),
        out_shape=(
            jax.ShapeDtypeStruct((order, order), jnp.float32),
            jax.ShapeDtypeStruct(matrix.shape, jnp.bfloat16),
        )
        + extra,
        in_specs=[VMEM] * 3,
        out_specs=(VMEM, pl.BlockSpec(memory_space=pltpu.HBM)) + (VMEM,) * len(extra),
        scratch_shapes=[
            pltpu.VMEM((order, order), jnp.float32),
            pltpu.VMEM((order, order), jnp.bfloat16),
            pltpu.VMEM(matrix.shape, jnp.bfloat16),
            pltpu.SemaphoreType.DMA((rows // 512,)),
        ],
        compiler_params=PARAMS,
        name=name,
    )(own, other, matrix)


def sum_all(kept, sent):
    swap = [(0, 1), (1, 0)]
    kept = kept + lax.ppermute(sent, "c", swap)
    count = lax.axis_size(CHIPS)
    parts = kept.reshape(count, kept.shape[0] // count // 2, 2, GB)
    parts = lax.all_to_all(parts, CHIPS, 0, 0, tiled=True)
    total = jnp.sum(parts, axis=0, keepdims=True)
    parts = jnp.broadcast_to(total, parts.shape)
    own = lax.all_to_all(parts, CHIPS, 0, 0, tiled=True).reshape(kept.shape)
    return own, lax.ppermute(own, "c", swap)


def on_device(panel, signs, sample_rows):
    n_had = lax.axis_size("z") * lax.axis_size("c")
    n_blk = lax.axis_size("x") * lax.axis_size("y")
    rows_dev, columns = panel.shape
    sketch_count = sample_rows.shape[1]
    signs = signs.reshape(1, rows_dev)
    sent = sketch_rows(False, sample_rows, signs, panel)
    other = lax.ppermute(sent, "c", [(0, 1), (1, 0)])
    mine = sketch_rows(True, sample_rows, signs, panel) + other
    chips = lax.axis_size(CHIPS)
    mine = mine.reshape(chips, sketch_count // 2 // chips, columns)
    parts = lax.all_to_all(mine, CHIPS, 0, 0, tiled=True)
    own, other = sum_all(*sketch_gram(parts))
    r_sketch, whitened, kept, sent = factor_and_apply(
        whiten_kernel, "whiten", (half_shape(columns),) * 2,
        1.0 / (n_had * LH * sketch_count * n_blk), own, other, panel,
    )
    own, other = sum_all(kept, sent)
    r_gram, q_panel = factor_and_apply(
        finish_kernel, "finish", (), 1.0 / (rows_dev * n_had * n_blk), own, other, whitened
    )
    return (q_panel, r_sketch, r_gram)


def solution(mesh):
    devices = mesh.devices.reshape(4, 2, 4, 4)
    split = Mesh(devices, AXES)
    placed = (P(AXES, None), P(AXES), P(("x", "y"), None))
    return jax.shard_map(
        on_device,
        mesh=split,
        in_specs=placed,
        out_specs=(P(AXES, None), P(), P()),
        check_vma=False,
    )
```

```python
import functools

import jax
import jax.numpy as jnp
from jax import lax
from jax.experimental import pallas as pl
from jax.experimental.pallas import tpu as pltpu
from jax.sharding import Mesh, PartitionSpec as P

LH = 32
NB = 64
GB = 128
AXES = ("z", "c", "x", "y")
CHIPS = ("z", "x", "y")
HIGHEST = lax.Precision.HIGHEST
VMEM = pl.BlockSpec(memory_space=pltpu.VMEM)
PARAMS = pltpu.CompilerParams(vmem_limit_bytes=48 * 1024 * 1024)


def dot(first, second, first_dim=1, second_dim=0, precision=None):
    return lax.dot_general(
        first,
        second,
        (((first_dim,), (second_dim,)), ((), ())),
        precision=precision,
        preferred_element_type=jnp.float32,
    )


def upper_blocks(columns):
    count = columns // GB
    return [(i, j) for i in range(count) for j in range(i, count)]


def parity(value):
    for shift in (4, 2, 1):
        value = jnp.bitwise_xor(value, jnp.right_shift(value, shift))
    return jnp.bitwise_and(value, 1)


def sketch_kernel(own_half, picks_ref, signs_ref, panel_ref, out_ref):
    rows = panel_ref.shape[0]
    group_mine = lax.axis_index("z") * lax.axis_size("c") + lax.axis_index("c")
    half = lax.axis_index("c") if own_half else 1 - lax.axis_index("c")
    lane = lax.broadcasted_iota(jnp.int32, (128, 128), 1)
    inner_lane = jnp.bitwise_and(lane, LH - 1)
    group_lane = lane // LH
    flips = (1 - 2 * signs_ref[...]).astype(jnp.float32)
    for chunk in range(out_ref.shape[0] // 256):
        strips = []
        for part in range(2):
            start = pl.multiple_of(half * out_ref.shape[0] + chunk * 256 + part * 128, 128)
            picks = jnp.broadcast_to(picks_ref[:, pl.ds(start, 128)], (128, 128)).T
            owners = jnp.right_shift(picks, rows.bit_length() - 1)
            bits = jnp.bitwise_and(jnp.bitwise_and(picks, LH - 1), inner_lane)
            bits = parity(jnp.bitwise_xor(bits, parity(jnp.bitwise_and(owners, group_mine))))
            values = (1 - 2 * bits).astype(jnp.float32)
            group = jnp.right_shift(jnp.bitwise_and(picks, rows - 1), 5) - group_lane
            strips.append((values, group))
        tiles = []
        for tile in range(rows // 128):
            flip = flips[:, tile * 128 : tile * 128 + 128]
            tiles.append(
                jnp.concatenate(
                    [jnp.where(group == 4 * tile, values * flip, 0.0).astype(jnp.bfloat16)
                     for values, group in strips],
                    axis=0,
                )
            )
        chosen = jnp.concatenate(tiles, axis=1)
        out_ref[chunk * 256 : chunk * 256 + 256, :] = dot(chosen, panel_ref[...])


def sketch_rows(own_half, picks, signs, panel):
    return pl.pallas_call(
        functools.partial(sketch_kernel, own_half),
        out_shape=jax.ShapeDtypeStruct((picks.shape[1] // 2, panel.shape[1]), jnp.float32),
        in_specs=[VMEM] * 3,
        out_specs=VMEM,
        compiler_params=PARAMS,
        name="sketch_own" if own_half else "sketch_sent",
    )(picks, signs, panel)


def pack_gram(matrix, kept_ref, sent_ref, precision):
    columns = matrix.shape[1]
    blocks = []
    for i in range(columns // GB):
        strip = dot(matrix[:, i * GB : i * GB + GB], matrix[:, i * GB :], 0, 0, precision)
        blocks += [strip[:, j * GB : j * GB + GB] for j in range(columns // GB - i)]
    first = lax.axis_index("c") == 0
    half = len(blocks) // 2
    for place in range(half):
        own = slice(place * GB, place * GB + GB)
        kept_ref[own, :] = jnp.where(first, blocks[place], blocks[place + half])
        sent_ref[own, :] = jnp.where(first, blocks[place + half], blocks[place])


def half_shape(columns):
    return jax.ShapeDtypeStruct((len(upper_blocks(columns)) // 2 * GB, GB), jnp.float32)


def sketch_gram_kernel(parts_ref, kept_ref, sent_ref):
    pack_gram(jnp.sum(parts_ref[...], axis=0), kept_ref, sent_ref, HIGHEST)


def sketch_gram(parts):
    columns = parts.shape[2]
    return pl.pallas_call(
        sketch_gram_kernel,
        out_shape=(half_shape(columns),) * 2,
        in_specs=[VMEM],
        out_specs=(VMEM, VMEM),
        compiler_params=PARAMS,
        name="sketch_gram",
    )(parts)


def times_inverse(rows_ref, inverse, buffer, out_ref, sems):
    rows, columns = rows_ref.shape
    half = columns // 2
    copies = []
    for place, start in enumerate(range(0, rows, 512)):
        own = pl.ds(start, 512)
        buffer[own, :half] = dot(
            rows_ref[own, :half], inverse[:half, :half], 1, 1
        ).astype(jnp.bfloat16)
        buffer[own, half:] = dot(rows_ref[own, :], inverse[half:, :], 1, 1).astype(jnp.bfloat16)
        copies.append(pltpu.make_async_copy(buffer.at[own, :], out_ref.at[own, :], sems.at[place]))
        copies[-1].start()
    return copies


def spread_row(tile, k):
    return jnp.broadcast_to(tile[k : k + 1, :], tile.shape)


def spread_lane(tile, c):
    return jnp.broadcast_to(tile[:, c : c + 1], tile.shape)


def factor_block(block):
    row = lax.broadcasted_iota(jnp.int32, (NB, NB), 0)
    column = lax.broadcasted_iota(jnp.int32, (NB, NB), 1)
    both = jnp.concatenate([block, (row == column).astype(jnp.float32)], axis=1)
    count = NB // 8
    work = [both[8 * u : 8 * u + 8, :] for u in range(count)]
    sub = lax.broadcasted_iota(jnp.int32, (8, 128), 0)
    done = []
    ahead = [spread_lane(work[0], c) for c in range(8)]
    for t in range(count):
        lanes = {u: [spread_lane(work[u], 8 * t + c) for c in range(8)] for u in range(t + 1, count)}
        lanes[t] = ahead
        if t + 1 < count:
            beside = [spread_lane(work[t], 8 * t + 8 + c) for c in range(8)]
            ahead = [spread_lane(work[t + 1], 8 * t + 8 + c) for c in range(8)]
        pivots = None
        for k in range(8):
            pivot = spread_row(lanes[t][k], k)
            inverse = 1.0 / pivot
            pivots = pivot if k == 0 else jnp.where(sub == k, pivot, pivots)
            across = {c: spread_row(lanes[t][c], k) for c in range(k + 1, 8)}
            pivot_row = spread_row(work[t], k)
            ratio = jnp.where(sub > k, lanes[t][k], 0.0) * inverse
            for c in range(k + 1, 8):
                lanes[t][c] = lanes[t][c] - ratio * across[c]
            if t + 1 < count:
                next_ratio = lanes[t + 1][k] * inverse
                for c in range(8):
                    entry = spread_row(beside[c], k)
                    beside[c] = beside[c] - ratio * entry
                    ahead[c] = ahead[c] - next_ratio * entry
            if k < 7:
                work[t] = work[t] - ratio * pivot_row
            for u in range(t + 1, count):
                ratio = lanes[u][k] * inverse
                for c in range(k + 1, 8):
                    lanes[u][c] = lanes[u][c] - ratio * across[c]
                work[u] = work[u] - ratio * pivot_row
        done.append(work[t] * lax.rsqrt(pivots))
    return jnp.concatenate(done, axis=0)


def split(value):
    first = value.astype(jnp.bfloat16)
    left = value - first.astype(jnp.float32)
    second = left.astype(jnp.bfloat16)
    third = (left - second.astype(jnp.float32)).astype(jnp.bfloat16)
    return first, second, third


def left_terms(value, axis):
    first, second, third = split(value)
    return jnp.concatenate([first, first, second, second, first, third], axis=axis)


def right_terms(value, axis):
    first, second, third = split(value)
    return jnp.concatenate([first, second, first, second, third, first], axis=axis)


def factor_into(scale, sum_ref, factor_ref, inverse_ref, work):
    order = work.shape[0]
    blocks = upper_blocks(order)
    half = len(blocks) // 2
    depth = lax.axis_size("z")
    piece = half * GB // depth
    for place, (i, j) in enumerate(blocks):
        side, row = divmod(place * GB, half * GB)
        end, target = row + GB, i * GB
        while row < end:
            level, within = divmod(row, piece)
            size = min(end - row, piece - within)
            source = (2 * level + side) * piece + within
            work[target : target + size, j * GB : j * GB + GB] = (
                sum_ref[source : source + size, :] * scale
            )
            row, target = row + size, target + size
        if i != j:
            work[j * GB : j * GB + GB, i * GB : i * GB + GB] = work[
                i * GB : i * GB + GB, j * GB : j * GB + GB
            ].T
    row = lax.broadcasted_iota(jnp.int32, (NB, NB), 0)
    column = lax.broadcasted_iota(jnp.int32, (NB, NB), 1)
    wide = lax.broadcasted_iota(jnp.int32, (NB, order), 1)
    for end in range(NB, order + 1, NB):
        own = slice(end - NB, end)
        rest = slice(end, order)
        both = factor_block(work[own, own])
        diagonal = jnp.where(row <= column, both[:, :NB], 0.0)
        inverse = left_terms(both[:, NB:], 1)
        if end < order:
            left = dot(right_terms(work[rest, own], 1), inverse, 1, 1)
        work[own, own] = (row == column).astype(jnp.float32)
        strip = dot(inverse, right_terms(work[own, :], 0))
        inverse_ref[own, :] = jnp.where(wide < end, strip, 0.0).astype(jnp.bfloat16)
        factor_ref[own, :] = jnp.where(wide >= end, strip, 0.0)
        factor_ref[own, own] = diagonal
        if end < order:
            work[rest, own] = jnp.zeros((order - end, NB), jnp.float32)
            work[rest, :] = work[rest, :] - dot(left_terms(left, 1), right_terms(strip, 0))


def whiten_kernel(
    scale, sum_ref, panel_ref, factor_ref, white_ref, kept_ref, sent_ref,
    work, inverse, buffer, sems,
):
    factor_into(scale, sum_ref, factor_ref, inverse, work)
    copies = times_inverse(panel_ref, inverse, buffer, white_ref, sems)
    pack_gram(buffer[...], kept_ref, sent_ref, None)
    for copy in copies:
        copy.wait()


def finish_kernel(
    scale, sum_ref, white_ref, factor_ref, out_ref, work, inverse, buffer, sems
):
    factor_into(scale, sum_ref, factor_ref, inverse, work)
    for copy in times_inverse(white_ref, inverse, buffer, out_ref, sems):
        copy.wait()


def factor_and_apply(kernel, name, extra, scale, summed, matrix):
    rows, order = matrix.shape
    return pl.pallas_call(
        functools.partial(kernel, scale),
        out_shape=(
            jax.ShapeDtypeStruct((order, order), jnp.float32),
            jax.ShapeDtypeStruct(matrix.shape, jnp.bfloat16),
        )
        + extra,
        in_specs=[VMEM] * 2,
        out_specs=(VMEM, pl.BlockSpec(memory_space=pltpu.HBM)) + (VMEM,) * len(extra),
        scratch_shapes=[
            pltpu.VMEM((order, order), jnp.float32),
            pltpu.VMEM((order, order), jnp.bfloat16),
            pltpu.VMEM(matrix.shape, jnp.bfloat16),
            pltpu.SemaphoreType.DMA((rows // 512,)),
        ],
        compiler_params=PARAMS,
        name=name,
    )(summed, matrix)


def sum_all(kept, sent):
    kept = kept + lax.ppermute(sent, "c", [(0, 1), (1, 0)])
    count = lax.axis_size(CHIPS)
    parts = kept.reshape(count, kept.shape[0] // count // 2, 2, GB)
    parts = lax.all_to_all(parts, CHIPS, 0, 0, tiled=True)
    total = jnp.sum(parts, axis=0, keepdims=True)
    parts = jnp.broadcast_to(total, (2 * count,) + parts.shape[1:])
    return lax.all_to_all(parts, AXES, 0, 0, tiled=True).reshape(2 * kept.shape[0], GB)


def on_device(panel, signs, sample_rows):
    n_had = lax.axis_size("z") * lax.axis_size("c")
    n_blk = lax.axis_size("x") * lax.axis_size("y")
    rows_dev, columns = panel.shape
    sketch_count = sample_rows.shape[1]
    signs = signs.reshape(1, rows_dev)
    sent = sketch_rows(False, sample_rows, signs, panel)
    other = lax.ppermute(sent, "c", [(0, 1), (1, 0)])
    mine = sketch_rows(True, sample_rows, signs, panel) + other
    chips = lax.axis_size(CHIPS)
    mine = mine.reshape(chips, sketch_count // 2 // chips, columns)
    parts = lax.all_to_all(mine, CHIPS, 0, 0, tiled=True)
    summed = sum_all(*sketch_gram(parts))
    r_sketch, whitened, kept, sent = factor_and_apply(
        whiten_kernel, "whiten", (half_shape(columns),) * 2,
        1.0 / (n_had * LH * sketch_count * n_blk), summed, panel,
    )
    summed = sum_all(kept, sent)
    r_gram, q_panel = factor_and_apply(
        finish_kernel, "finish", (), 1.0 / (rows_dev * n_had * n_blk), summed, whitened
    )
    return (q_panel, r_sketch, r_gram)


def solution(mesh):
    devices = mesh.devices.reshape(4, 2, 4, 4)
    split = Mesh(devices, AXES)
    placed = (P(AXES, None), P(AXES), P(("x", "y"), None))
    return jax.shard_map(
        on_device,
        mesh=split,
        in_specs=placed,
        out_specs=(P(AXES, None), P(), P()),
        check_vma=False,
    )
```

```python
import functools

import jax
import jax.numpy as jnp
from jax import lax
from jax.experimental import pallas as pl
from jax.experimental.pallas import tpu as pltpu
from jax.sharding import Mesh, PartitionSpec as P

LH = 32
NB = 64
GB = 128
AXES = ("z", "c", "x", "y")
CHIPS = ("z", "x", "y")
HIGHEST = lax.Precision.HIGHEST
VMEM = pl.BlockSpec(memory_space=pltpu.VMEM)
PARAMS = pltpu.CompilerParams(vmem_limit_bytes=48 * 1024 * 1024)


def dot(first, second, first_dim=1, second_dim=0, precision=None):
    return lax.dot_general(
        first,
        second,
        (((first_dim,), (second_dim,)), ((), ())),
        precision=precision,
        preferred_element_type=jnp.float32,
    )


def upper_blocks(columns):
    count = columns // GB
    return [(i, j) for i in range(count) for j in range(i, count)]


def parity(value):
    for shift in (4, 2, 1):
        value = jnp.bitwise_xor(value, jnp.right_shift(value, shift))
    return jnp.bitwise_and(value, 1)


def sketch_kernel(own_half, picks_ref, signs_ref, panel_ref, out_ref):
    rows = panel_ref.shape[0]
    group_mine = lax.axis_index("z") * lax.axis_size("c") + lax.axis_index("c")
    half = lax.axis_index("c") if own_half else 1 - lax.axis_index("c")
    lane = lax.broadcasted_iota(jnp.int32, (128, 128), 1)
    inner_lane = jnp.bitwise_and(lane, LH - 1)
    group_lane = lane // LH
    flips = (1 - 2 * signs_ref[...]).astype(jnp.float32)
    for chunk in range(out_ref.shape[0] // 256):
        strips = []
        for part in range(2):
            start = pl.multiple_of(half * out_ref.shape[0] + chunk * 256 + part * 128, 128)
            picks = jnp.broadcast_to(picks_ref[:, pl.ds(start, 128)], (128, 128)).T
            owners = jnp.right_shift(picks, rows.bit_length() - 1)
            bits = jnp.bitwise_and(jnp.bitwise_and(picks, LH - 1), inner_lane)
            bits = parity(jnp.bitwise_xor(bits, parity(jnp.bitwise_and(owners, group_mine))))
            values = (1 - 2 * bits).astype(jnp.float32)
            group = jnp.right_shift(jnp.bitwise_and(picks, rows - 1), 5) - group_lane
            strips.append((values, group))
        tiles = []
        for tile in range(rows // 128):
            flip = flips[:, tile * 128 : tile * 128 + 128]
            tiles.append(
                jnp.concatenate(
                    [jnp.where(group == 4 * tile, values * flip, 0.0).astype(jnp.bfloat16)
                     for values, group in strips],
                    axis=0,
                )
            )
        chosen = jnp.concatenate(tiles, axis=1)
        out_ref[chunk * 256 : chunk * 256 + 256, :] = dot(chosen, panel_ref[...])


def sketch_rows(own_half, picks, signs, panel):
    return pl.pallas_call(
        functools.partial(sketch_kernel, own_half),
        out_shape=jax.ShapeDtypeStruct((picks.shape[1] // 2, panel.shape[1]), jnp.float32),
        in_specs=[VMEM] * 3,
        out_specs=VMEM,
        compiler_params=PARAMS,
        name="sketch_own" if own_half else "sketch_sent",
    )(picks, signs, panel)


def pack_gram(matrix, kept_ref, sent_ref, precision):
    columns = matrix.shape[1]
    blocks = []
    for i in range(columns // GB):
        strip = dot(matrix[:, i * GB : i * GB + GB], matrix[:, i * GB :], 0, 0, precision)
        blocks += [strip[:, j * GB : j * GB + GB] for j in range(columns // GB - i)]
    first = lax.axis_index("c") == 0
    half = len(blocks) // 2
    for place in range(half):
        own = slice(place * GB, place * GB + GB)
        kept_ref[own, :] = jnp.where(first, blocks[place], blocks[place + half])
        sent_ref[own, :] = jnp.where(first, blocks[place + half], blocks[place])


def half_shape(columns):
    return jax.ShapeDtypeStruct((len(upper_blocks(columns)) // 2 * GB, GB), jnp.float32)


def sketch_gram_kernel(parts_ref, kept_ref, sent_ref):
    pack_gram(jnp.sum(parts_ref[...], axis=0), kept_ref, sent_ref, HIGHEST)


def sketch_gram(parts):
    columns = parts.shape[2]
    return pl.pallas_call(
        sketch_gram_kernel,
        out_shape=(half_shape(columns),) * 2,
        in_specs=[VMEM],
        out_specs=(VMEM, VMEM),
        compiler_params=PARAMS,
        name="sketch_gram",
    )(parts)


def times_inverse(rows_ref, inverse, buffer, out_ref, sems):
    rows, columns = rows_ref.shape
    half = columns // 2
    copies = []
    for place, start in enumerate(range(0, rows, 512)):
        own = pl.ds(start, 512)
        buffer[own, :half] = dot(
            rows_ref[own, :half], inverse[:half, :half], 1, 1
        ).astype(jnp.bfloat16)
        buffer[own, half:] = dot(rows_ref[own, :], inverse[half:, :], 1, 1).astype(jnp.bfloat16)
        copies.append(pltpu.make_async_copy(buffer.at[own, :], out_ref.at[own, :], sems.at[place]))
        copies[-1].start()
    return copies


def spread_row(tile, k):
    return jnp.broadcast_to(tile[k : k + 1, :], tile.shape)


def spread_lane(tile, c):
    return jnp.broadcast_to(tile[:, c : c + 1], tile.shape)


def factor_block(block):
    row = lax.broadcasted_iota(jnp.int32, (NB, NB), 0)
    column = lax.broadcasted_iota(jnp.int32, (NB, NB), 1)
    both = jnp.concatenate([block, (row == column).astype(jnp.float32)], axis=1)
    count = NB // 8
    work = [both[8 * u : 8 * u + 8, :] for u in range(count)]
    sub = lax.broadcasted_iota(jnp.int32, (8, 128), 0)
    done = []
    ahead = [spread_lane(work[0], c) for c in range(8)]
    for t in range(count):
        lanes = {u: [spread_lane(work[u], 8 * t + c) for c in range(8)] for u in range(t + 1, count)}
        lanes[t] = ahead
        if t + 1 < count:
            beside = [spread_lane(work[t], 8 * t + 8 + c) for c in range(8)]
            ahead = [spread_lane(work[t + 1], 8 * t + 8 + c) for c in range(8)]
        pivots = None
        for k in range(8):
            pivot = spread_row(lanes[t][k], k)
            inverse = 1.0 / pivot
            pivots = pivot if k == 0 else jnp.where(sub == k, pivot, pivots)
            across = {c: spread_row(lanes[t][c], k) for c in range(k + 1, 8)}
            pivot_row = spread_row(work[t], k)
            ratio = jnp.where(sub > k, lanes[t][k], 0.0) * inverse
            for c in range(k + 1, 8):
                lanes[t][c] = lanes[t][c] - ratio * across[c]
            if t + 1 < count:
                next_ratio = lanes[t + 1][k] * inverse
                for c in range(8):
                    entry = spread_row(beside[c], k)
                    beside[c] = beside[c] - ratio * entry
                    ahead[c] = ahead[c] - next_ratio * entry
            if k < 7:
                work[t] = work[t] - ratio * pivot_row
            for u in range(t + 1, count):
                ratio = lanes[u][k] * inverse
                for c in range(k + 1, 8):
                    lanes[u][c] = lanes[u][c] - ratio * across[c]
                work[u] = work[u] - ratio * pivot_row
        done.append(work[t] * lax.rsqrt(pivots))
    return jnp.concatenate(done, axis=0)


def split(value):
    first = value.astype(jnp.bfloat16)
    left = value - first.astype(jnp.float32)
    second = left.astype(jnp.bfloat16)
    third = (left - second.astype(jnp.float32)).astype(jnp.bfloat16)
    return first, second, third


def left_terms(value, axis):
    first, second, third = split(value)
    return jnp.concatenate([first, first, second, second, first, third], axis=axis)


def right_terms(value, axis):
    first, second, third = split(value)
    return jnp.concatenate([first, second, first, second, third, first], axis=axis)


def factor_into(scale, own_ref, other_ref, factor_ref, inverse_ref, work):
    order = work.shape[0]
    first = lax.axis_index("c") == 0
    blocks = upper_blocks(order)
    half = len(blocks) // 2
    for place in range(half):
        rows = slice(place * GB, place * GB + GB)
        own, other = own_ref[rows, :] * scale, other_ref[rows, :] * scale
        for which, block in (
            (place, jnp.where(first, own, other)),
            (place + half, jnp.where(first, other, own)),
        ):
            i, j = blocks[which]
            work[i * GB : i * GB + GB, j * GB : j * GB + GB] = block
            if i != j:
                work[j * GB : j * GB + GB, i * GB : i * GB + GB] = block.T
    eliminate(factor_ref, inverse_ref, work)


def times(first, second, first_dim=1, second_dim=0):
    return dot(left_terms(first, first_dim), right_terms(second, second_dim), first_dim, second_dim)


def factor_pair(block):
    row = lax.broadcasted_iota(jnp.int32, (NB, NB), 0)
    column = lax.broadcasted_iota(jnp.int32, (NB, NB), 1)
    zero = jnp.zeros((NB, NB), jnp.float32)
    first = factor_block(block[:NB, :NB])
    first_factor = jnp.where(row <= column, first[:, :NB], 0.0)
    first_inverse = first[:, NB:]
    above = times(first_inverse, block[:NB, NB:])
    below = times(block[NB:, :NB], first_inverse, 1, 1)
    second = factor_block(block[NB:, NB:] - times(below, above))
    second_factor = jnp.where(row <= column, second[:, :NB], 0.0)
    second_inverse = second[:, NB:]
    corner = -times(second_inverse, times(below, first_inverse))
    factor = jnp.concatenate(
        [jnp.concatenate([first_factor, above], axis=1), jnp.concatenate([zero, second_factor], axis=1)],
        axis=0,
    )
    inverse = jnp.concatenate(
        [jnp.concatenate([first_inverse, zero], axis=1), jnp.concatenate([corner, second_inverse], axis=1)],
        axis=0,
    )
    return factor, inverse


def eliminate(factor_ref, inverse_ref, work):
    order = work.shape[0]
    size = 2 * NB
    row = lax.broadcasted_iota(jnp.int32, (size, size), 0)
    column = lax.broadcasted_iota(jnp.int32, (size, size), 1)
    wide = lax.broadcasted_iota(jnp.int32, (size, order), 1)

    def apply(start, diagonal, inverse):
        own, rest = slice(start, start + size), slice(start + size, order)
        if start + size < order:
            left = dot(right_terms(work[rest, own], 1), inverse, 1, 1)
        work[own, own] = (row == column).astype(jnp.float32)
        strip = dot(inverse, right_terms(work[own, :], 0))
        inverse_ref[own, :] = jnp.where(wide < start + size, strip, 0.0).astype(jnp.bfloat16)
        factor_ref[own, :] = jnp.where(wide >= start + size, strip, 0.0)
        factor_ref[own, own] = diagonal
        if start + size < order:
            work[rest, own] = jnp.zeros((order - start - size, size), jnp.float32)
            work[rest, :] = work[rest, :] - dot(left_terms(left, 1), right_terms(strip, 0))

    def step(place, carry):
        own = pl.ds(pl.multiple_of(place * size, size), size)
        diagonal, inverse = factor_pair(work[own, own])
        inverse = left_terms(inverse, 1)
        for start in range(0, order, size):
            pl.when(place * size == start)(functools.partial(apply, start, diagonal, inverse))
        return carry

    lax.fori_loop(0, order // size, step, 0)


def whiten_kernel(
    scale, own_ref, other_ref, panel_ref, factor_ref, white_ref, kept_ref, sent_ref,
    work, inverse, buffer, sems,
):
    factor_into(scale, own_ref, other_ref, factor_ref, inverse, work)
    copies = times_inverse(panel_ref, inverse, buffer, white_ref, sems)
    pack_gram(buffer[...], kept_ref, sent_ref, None)
    for copy in copies:
        copy.wait()


def finish_kernel(
    scale, own_ref, other_ref, white_ref, factor_ref, out_ref, work, inverse, buffer, sems
):
    factor_into(scale, own_ref, other_ref, factor_ref, inverse, work)
    for copy in times_inverse(white_ref, inverse, buffer, out_ref, sems):
        copy.wait()


def factor_and_apply(kernel, name, extra, scale, own, other, matrix):
    rows, order = matrix.shape
    return pl.pallas_call(
        functools.partial(kernel, scale),
        out_shape=(
            jax.ShapeDtypeStruct((order, order), jnp.float32),
            jax.ShapeDtypeStruct(matrix.shape, jnp.bfloat16),
        )
        + extra,
        in_specs=[VMEM] * 3,
        out_specs=(VMEM, pl.BlockSpec(memory_space=pltpu.HBM)) + (VMEM,) * len(extra),
        scratch_shapes=[
            pltpu.VMEM((order, order), jnp.float32),
            pltpu.VMEM((order, order), jnp.bfloat16),
            pltpu.VMEM(matrix.shape, jnp.bfloat16),
            pltpu.SemaphoreType.DMA((rows // 512,)),
        ],
        compiler_params=PARAMS,
        name=name,
    )(own, other, matrix)


def sum_all(kept, sent):
    swap = [(0, 1), (1, 0)]
    kept = kept + lax.ppermute(sent, "c", swap)
    count = lax.axis_size(CHIPS)
    parts = kept.reshape(count, kept.shape[0] // count // 2, 2, GB)
    parts = lax.all_to_all(parts, CHIPS, 0, 0, tiled=True)
    total = jnp.sum(parts, axis=0, keepdims=True)
    parts = jnp.broadcast_to(total, parts.shape)
    own = lax.all_to_all(parts, CHIPS, 0, 0, tiled=True).reshape(kept.shape)
    return own, lax.ppermute(own, "c", swap)


def on_device(panel, signs, sample_rows):
    n_had = lax.axis_size("z") * lax.axis_size("c")
    n_blk = lax.axis_size("x") * lax.axis_size("y")
    rows_dev, columns = panel.shape
    sketch_count = sample_rows.shape[1]
    signs = signs.reshape(1, rows_dev)
    sent = sketch_rows(False, sample_rows, signs, panel)
    other = lax.ppermute(sent, "c", [(0, 1), (1, 0)])
    mine = sketch_rows(True, sample_rows, signs, panel) + other
    chips = lax.axis_size(CHIPS)
    mine = mine.reshape(chips, sketch_count // 2 // chips, columns)
    parts = lax.all_to_all(mine, CHIPS, 0, 0, tiled=True)
    own, other = sum_all(*sketch_gram(parts))
    r_sketch, whitened, kept, sent = factor_and_apply(
        whiten_kernel, "whiten", (half_shape(columns),) * 2,
        1.0 / (n_had * LH * sketch_count * n_blk), own, other, panel,
    )
    own, other = sum_all(kept, sent)
    r_gram, q_panel = factor_and_apply(
        finish_kernel, "finish", (), 1.0 / (rows_dev * n_had * n_blk), own, other, whitened
    )
    return (q_panel, r_sketch, r_gram)


def solution(mesh):
    devices = mesh.devices.reshape(4, 2, 4, 4)
    split = Mesh(devices, AXES)
    placed = (P(AXES, None), P(AXES), P(("x", "y"), None))
    return jax.shard_map(
        on_device,
        mesh=split,
        in_specs=placed,
        out_specs=(P(AXES, None), P(), P()),
        check_vma=False,
    )
```

```python
import functools

import jax
import jax.numpy as jnp
from jax import lax
from jax.experimental import pallas as pl
from jax.experimental.pallas import tpu as pltpu
from jax.sharding import Mesh, PartitionSpec as P

LH = 32
NB = 64
GB = 128
AXES = ("z", "c", "x", "y")
CHIPS = ("z", "x", "y")
HIGHEST = lax.Precision.HIGHEST
VMEM = pl.BlockSpec(memory_space=pltpu.VMEM)
PARAMS = pltpu.CompilerParams(vmem_limit_bytes=48 * 1024 * 1024)


def dot(first, second, first_dim=1, second_dim=0, precision=None):
    return lax.dot_general(
        first,
        second,
        (((first_dim,), (second_dim,)), ((), ())),
        precision=precision,
        preferred_element_type=jnp.float32,
    )


def upper_blocks(columns):
    count = columns // GB
    return [(i, j) for i in range(count) for j in range(i, count)]


def parity(value):
    for shift in (4, 2, 1):
        value = jnp.bitwise_xor(value, jnp.right_shift(value, shift))
    return jnp.bitwise_and(value, 1)


def choice(own_half, count, picks_ref, signs_ref, chunk):
    rows = signs_ref.shape[1]
    group_mine = lax.axis_index("z") * lax.axis_size("c") + lax.axis_index("c")
    half = lax.axis_index("c") if own_half else 1 - lax.axis_index("c")
    lane = lax.broadcasted_iota(jnp.int32, (128, 128), 1)
    inner_lane = jnp.bitwise_and(lane, LH - 1)
    group_lane = lane // LH
    flips = (1 - 2 * signs_ref[...]).astype(jnp.float32)
    strips = []
    for part in range(2):
        start = pl.multiple_of(half * count + chunk * 256 + part * 128, 128)
        picks = jnp.broadcast_to(picks_ref[:, pl.ds(start, 128)], (128, 128)).T
        owners = jnp.right_shift(picks, rows.bit_length() - 1)
        bits = jnp.bitwise_and(jnp.bitwise_and(picks, LH - 1), inner_lane)
        bits = parity(jnp.bitwise_xor(bits, parity(jnp.bitwise_and(owners, group_mine))))
        values = (1 - 2 * bits).astype(jnp.float32)
        group = jnp.right_shift(jnp.bitwise_and(picks, rows - 1), 5) - group_lane
        strips.append((values, group))
    tiles = []
    for tile in range(rows // 128):
        flip = flips[:, tile * 128 : tile * 128 + 128]
        tiles.append(
            jnp.concatenate(
                [jnp.where(group == 4 * tile, values * flip, 0.0).astype(jnp.bfloat16)
                 for values, group in strips],
                axis=0,
            )
        )
    return jnp.concatenate(tiles, axis=1)


def sketch_sent_kernel(
    picks_hbm, signs_hbm, panel_hbm, out_ref, picks_ref, signs_ref, panel_ref, chosen, sems
):
    copies = [
        pltpu.make_async_copy(source, target, sems.at[place])
        for place, (source, target) in enumerate(
            ((picks_hbm, picks_ref), (signs_hbm, signs_ref), (panel_hbm, panel_ref))
        )
    ]
    for copy in copies:
        copy.start()
    copies[0].wait()
    copies[1].wait()
    count = out_ref.shape[0]
    for chunk in range(count // 256):
        chosen[chunk * 256 : chunk * 256 + 256, :] = choice(
            False, count, picks_ref, signs_ref, chunk
        )
    copies[2].wait()
    for start in range(0, count, 256):
        out_ref[start : start + 256, :] = dot(chosen[start : start + 256, :], panel_ref[...])


def sketch_own_kernel(picks_ref, signs_ref, panel_ref, out_ref):
    count = out_ref.shape[0]
    for chunk in range(count // 256):
        out_ref[chunk * 256 : chunk * 256 + 256, :] = dot(
            choice(True, count, picks_ref, signs_ref, chunk), panel_ref[...]
        )


def sketch_sent(picks, signs, panel):
    count, (rows, columns) = picks.shape[1] // 2, panel.shape
    return pl.pallas_call(
        sketch_sent_kernel,
        out_shape=(
            jax.ShapeDtypeStruct((count, columns), jnp.float32),
            jax.ShapeDtypeStruct(picks.shape, picks.dtype),
            jax.ShapeDtypeStruct(signs.shape, signs.dtype),
            jax.ShapeDtypeStruct(panel.shape, panel.dtype),
        ),
        in_specs=[pl.BlockSpec(memory_space=pltpu.HBM)] * 3,
        out_specs=(VMEM,) * 4,
        scratch_shapes=[
            pltpu.VMEM((count, rows), jnp.bfloat16),
            pltpu.SemaphoreType.DMA((3,)),
        ],
        compiler_params=PARAMS,
        name="sketch_sent",
    )(picks, signs, panel)


def sketch_own(picks, signs, panel):
    return pl.pallas_call(
        sketch_own_kernel,
        out_shape=jax.ShapeDtypeStruct((picks.shape[1] // 2, panel.shape[1]), jnp.float32),
        in_specs=[VMEM] * 3,
        out_specs=VMEM,
        compiler_params=PARAMS,
        name="sketch_own",
    )(picks, signs, panel)


def pack_gram(matrix, kept_ref, sent_ref, precision):
    columns = matrix.shape[1]
    blocks = []
    for i in range(columns // GB):
        strip = dot(matrix[:, i * GB : i * GB + GB], matrix[:, i * GB :], 0, 0, precision)
        blocks += [strip[:, j * GB : j * GB + GB] for j in range(columns // GB - i)]
    first = lax.axis_index("c") == 0
    half = len(blocks) // 2
    for place in range(half):
        own = slice(place * GB, place * GB + GB)
        kept_ref[own, :] = jnp.where(first, blocks[place], blocks[place + half])
        sent_ref[own, :] = jnp.where(first, blocks[place + half], blocks[place])


def half_shape(columns):
    return jax.ShapeDtypeStruct((len(upper_blocks(columns)) // 2 * GB, GB), jnp.float32)


def sketch_gram_kernel(parts_ref, kept_ref, sent_ref):
    pack_gram(jnp.sum(parts_ref[...], axis=0), kept_ref, sent_ref, HIGHEST)


def sketch_gram(parts):
    columns = parts.shape[2]
    return pl.pallas_call(
        sketch_gram_kernel,
        out_shape=(half_shape(columns),) * 2,
        in_specs=[VMEM],
        out_specs=(VMEM, VMEM),
        compiler_params=PARAMS,
        name="sketch_gram",
    )(parts)


def times_inverse(rows_ref, inverse, buffer, out_ref, sems):
    rows, columns = rows_ref.shape
    half = columns // 2
    copies = []
    for place, start in enumerate(range(0, rows, 512)):
        own = pl.ds(start, 512)
        buffer[own, :half] = dot(
            rows_ref[own, :half], inverse[:half, :half], 1, 1
        ).astype(jnp.bfloat16)
        buffer[own, half:] = dot(rows_ref[own, :], inverse[half:, :], 1, 1).astype(jnp.bfloat16)
        copies.append(pltpu.make_async_copy(buffer.at[own, :], out_ref.at[own, :], sems.at[place]))
        copies[-1].start()
    return copies


def spread_row(tile, k):
    return jnp.broadcast_to(tile[k : k + 1, :], tile.shape)


def spread_lane(tile, c):
    return jnp.broadcast_to(tile[:, c : c + 1], tile.shape)


def factor_block(block):
    row = lax.broadcasted_iota(jnp.int32, (NB, NB), 0)
    column = lax.broadcasted_iota(jnp.int32, (NB, NB), 1)
    both = jnp.concatenate([block, (row == column).astype(jnp.float32)], axis=1)
    count = NB // 8
    work = [both[8 * u : 8 * u + 8, :] for u in range(count)]
    sub = lax.broadcasted_iota(jnp.int32, (8, 128), 0)
    done = []
    ahead = [spread_lane(work[0], c) for c in range(8)]
    for t in range(count):
        lanes = {u: [spread_lane(work[u], 8 * t + c) for c in range(8)] for u in range(t + 1, count)}
        lanes[t] = ahead
        if t + 1 < count:
            beside = [spread_lane(work[t], 8 * t + 8 + c) for c in range(8)]
            ahead = [spread_lane(work[t + 1], 8 * t + 8 + c) for c in range(8)]
        pivots = None
        for k in range(8):
            pivot = spread_row(lanes[t][k], k)
            inverse = 1.0 / pivot
            pivots = pivot if k == 0 else jnp.where(sub == k, pivot, pivots)
            across = {c: spread_row(lanes[t][c], k) for c in range(k + 1, 8)}
            pivot_row = spread_row(work[t], k)
            ratio = jnp.where(sub > k, lanes[t][k], 0.0) * inverse
            for c in range(k + 1, 8):
                lanes[t][c] = lanes[t][c] - ratio * across[c]
            if t + 1 < count:
                next_ratio = lanes[t + 1][k] * inverse
                for c in range(8):
                    entry = spread_row(beside[c], k)
                    beside[c] = beside[c] - ratio * entry
                    ahead[c] = ahead[c] - next_ratio * entry
            if k < 7:
                work[t] = work[t] - ratio * pivot_row
            for u in range(t + 1, count):
                ratio = lanes[u][k] * inverse
                for c in range(k + 1, 8):
                    lanes[u][c] = lanes[u][c] - ratio * across[c]
                work[u] = work[u] - ratio * pivot_row
        done.append(work[t] * lax.rsqrt(pivots))
    return jnp.concatenate(done, axis=0)


def split(value):
    first = value.astype(jnp.bfloat16)
    left = value - first.astype(jnp.float32)
    second = left.astype(jnp.bfloat16)
    third = (left - second.astype(jnp.float32)).astype(jnp.bfloat16)
    return first, second, third


def left_terms(value, axis):
    first, second, third = split(value)
    return jnp.concatenate([first, first, second, second, first, third], axis=axis)


def right_terms(value, axis):
    first, second, third = split(value)
    return jnp.concatenate([first, second, first, second, third, first], axis=axis)


def factor_into(scale, own_ref, other_ref, factor_ref, inverse_ref, work):
    order = work.shape[0]
    first = lax.axis_index("c") == 0
    blocks = upper_blocks(order)
    half = len(blocks) // 2
    for place in range(half):
        rows = slice(place * GB, place * GB + GB)
        own, other = own_ref[rows, :] * scale, other_ref[rows, :] * scale
        for which, block in (
            (place, jnp.where(first, own, other)),
            (place + half, jnp.where(first, other, own)),
        ):
            i, j = blocks[which]
            work[i * GB : i * GB + GB, j * GB : j * GB + GB] = block
            if i != j:
                work[j * GB : j * GB + GB, i * GB : i * GB + GB] = block.T
    eliminate(factor_ref, inverse_ref, work)


def times(first, second, first_dim=1, second_dim=0):
    return dot(left_terms(first, first_dim), right_terms(second, second_dim), first_dim, second_dim)


def factor_pair(block):
    row = lax.broadcasted_iota(jnp.int32, (NB, NB), 0)
    column = lax.broadcasted_iota(jnp.int32, (NB, NB), 1)
    zero = jnp.zeros((NB, NB), jnp.float32)
    first = factor_block(block[:NB, :NB])
    first_factor = jnp.where(row <= column, first[:, :NB], 0.0)
    first_inverse = first[:, NB:]
    above = times(first_inverse, block[:NB, NB:])
    below = times(block[NB:, :NB], first_inverse, 1, 1)
    second = factor_block(block[NB:, NB:] - times(below, above))
    second_factor = jnp.where(row <= column, second[:, :NB], 0.0)
    second_inverse = second[:, NB:]
    corner = -times(second_inverse, times(below, first_inverse))
    factor = jnp.concatenate(
        [jnp.concatenate([first_factor, above], axis=1), jnp.concatenate([zero, second_factor], axis=1)],
        axis=0,
    )
    inverse = jnp.concatenate(
        [jnp.concatenate([first_inverse, zero], axis=1), jnp.concatenate([corner, second_inverse], axis=1)],
        axis=0,
    )
    return factor, inverse


def eliminate(factor_ref, inverse_ref, work):
    order = work.shape[0]
    size = 2 * NB
    row = lax.broadcasted_iota(jnp.int32, (size, size), 0)
    column = lax.broadcasted_iota(jnp.int32, (size, size), 1)
    wide = lax.broadcasted_iota(jnp.int32, (size, order), 1)

    def apply(start, diagonal, inverse):
        own, rest = slice(start, start + size), slice(start + size, order)
        if start + size < order:
            left = dot(right_terms(work[rest, own], 1), inverse, 1, 1)
        work[own, own] = (row == column).astype(jnp.float32)
        strip = dot(inverse, right_terms(work[own, :], 0))
        inverse_ref[own, :] = jnp.where(wide < start + size, strip, 0.0).astype(jnp.bfloat16)
        factor_ref[own, :] = jnp.where(wide >= start + size, strip, 0.0)
        factor_ref[own, own] = diagonal
        if start + size < order:
            work[rest, own] = jnp.zeros((order - start - size, size), jnp.float32)
            work[rest, :] = work[rest, :] - dot(left_terms(left, 1), right_terms(strip, 0))

    def step(place, carry):
        own = pl.ds(pl.multiple_of(place * size, size), size)
        diagonal, inverse = factor_pair(work[own, own])
        inverse = left_terms(inverse, 1)
        for start in range(0, order, size):
            pl.when(place * size == start)(functools.partial(apply, start, diagonal, inverse))
        return carry

    lax.fori_loop(0, order // size, step, 0)


def whiten_kernel(
    scale, own_ref, other_ref, panel_ref, factor_ref, white_ref, kept_ref, sent_ref,
    work, inverse, buffer, sems,
):
    factor_into(scale, own_ref, other_ref, factor_ref, inverse, work)
    copies = times_inverse(panel_ref, inverse, buffer, white_ref, sems)
    pack_gram(buffer[...], kept_ref, sent_ref, None)
    for copy in copies:
        copy.wait()


def finish_kernel(
    scale, own_ref, other_ref, white_hbm, factor_ref, out_ref, work, inverse, buffer, sems, white_ref, arrived
):
    arrival = pltpu.make_async_copy(white_hbm.at[pl.ds(0, white_ref.shape[0]), :], white_ref, arrived)
    arrival.start()
    factor_into(scale, own_ref, other_ref, factor_ref, inverse, work)
    arrival.wait()
    for copy in times_inverse(white_ref, inverse, buffer, out_ref, sems):
        copy.wait()


HBM = pl.BlockSpec(memory_space=pltpu.HBM)
STRETCH = 16


def scratch(rows, order):
    return [
        pltpu.VMEM((order, order), jnp.float32),
        pltpu.VMEM((order, order), jnp.bfloat16),
        pltpu.VMEM((rows, order), jnp.bfloat16),
        pltpu.SemaphoreType.DMA((rows // 512,)),
    ]


def whiten(scale, own, other, panel):
    rows, order = panel.shape
    return pl.pallas_call(
        functools.partial(whiten_kernel, scale),
        out_shape=(
            jax.ShapeDtypeStruct((order, order), jnp.float32),
            jax.ShapeDtypeStruct((STRETCH * rows, order), jnp.bfloat16),
            half_shape(order),
            half_shape(order),
        ),
        in_specs=[VMEM] * 3,
        out_specs=(VMEM, HBM, VMEM, VMEM),
        scratch_shapes=scratch(rows, order),
        compiler_params=PARAMS,
        name="whiten",
    )(own, other, panel)


def finish(scale, own, other, whitened):
    rows, order = whitened.shape[0] // STRETCH, whitened.shape[1]
    return pl.pallas_call(
        functools.partial(finish_kernel, scale),
        out_shape=(
            jax.ShapeDtypeStruct((order, order), jnp.float32),
            jax.ShapeDtypeStruct((rows, order), jnp.bfloat16),
        ),
        in_specs=[VMEM, VMEM, HBM],
        out_specs=(VMEM, HBM),
        scratch_shapes=scratch(rows, order)
        + [pltpu.VMEM((rows, order), jnp.bfloat16), pltpu.SemaphoreType.DMA],
        compiler_params=PARAMS,
        name="finish",
    )(own, other, whitened)


def sum_all(kept, sent):
    swap = [(0, 1), (1, 0)]
    kept = kept + lax.ppermute(sent, "c", swap)
    count = lax.axis_size(CHIPS)
    parts = kept.reshape(count, kept.shape[0] // count // 2, 2, GB)
    parts = lax.all_to_all(parts, CHIPS, 0, 0, tiled=True)
    total = jnp.sum(parts, axis=0, keepdims=True)
    parts = jnp.broadcast_to(total, parts.shape)
    own = lax.all_to_all(parts, CHIPS, 0, 0, tiled=True).reshape(kept.shape)
    return own, lax.ppermute(own, "c", swap)


def on_device(panel, signs, sample_rows):
    n_had = lax.axis_size("z") * lax.axis_size("c")
    n_blk = lax.axis_size("x") * lax.axis_size("y")
    rows_dev, columns = panel.shape
    sketch_count = sample_rows.shape[1]
    signs = signs.reshape(1, rows_dev)
    sent, picks_near, signs_near, panel_near = sketch_sent(sample_rows, signs, panel)
    other = lax.ppermute(sent, "c", [(0, 1), (1, 0)])
    mine = sketch_own(picks_near, signs_near, panel_near) + other
    chips = lax.axis_size(CHIPS)
    mine = mine.reshape(chips, sketch_count // 2 // chips, columns)
    parts = lax.all_to_all(mine, CHIPS, 0, 0, tiled=True)
    own, other = sum_all(*sketch_gram(parts))
    r_sketch, whitened, kept, sent = whiten(
        1.0 / (n_had * LH * sketch_count * n_blk), own, other, panel
    )
    own, other = sum_all(kept, sent)
    r_gram, q_panel = finish(1.0 / (rows_dev * n_had * n_blk), own, other, whitened)
    return (q_panel, r_sketch, r_gram)


def solution(mesh):
    devices = mesh.devices.reshape(4, 2, 4, 4)
    split = Mesh(devices, AXES)
    placed = (P(AXES, None), P(AXES), P(("x", "y"), None))
    return jax.shard_map(
        on_device,
        mesh=split,
        in_specs=placed,
        out_specs=(P(AXES, None), P(), P()),
        check_vma=False,
    )
```

```python
import functools

import jax
import jax.numpy as jnp
from jax import lax
from jax.experimental import pallas as pl
from jax.experimental.pallas import tpu as pltpu
from jax.sharding import Mesh, PartitionSpec as P

LH = 32
NB = 64
GB = 128
AXES = ("z", "c", "x", "y")
CHIPS = ("z", "x", "y")
HIGHEST = lax.Precision.HIGHEST
VMEM = pl.BlockSpec(memory_space=pltpu.VMEM)
PARAMS = pltpu.CompilerParams(vmem_limit_bytes=48 * 1024 * 1024)


def dot(first, second, first_dim=1, second_dim=0, precision=None):
    return lax.dot_general(
        first,
        second,
        (((first_dim,), (second_dim,)), ((), ())),
        precision=precision,
        preferred_element_type=jnp.float32,
    )


def upper_blocks(columns):
    count = columns // GB
    return [(i, j) for i in range(count) for j in range(i, count)]


def parity(value):
    for shift in (4, 2, 1):
        value = jnp.bitwise_xor(value, jnp.right_shift(value, shift))
    return jnp.bitwise_and(value, 1)


def choice(own_half, count, picks_ref, signs_ref, chunk):
    rows = signs_ref.shape[1]
    group_mine = lax.axis_index("z") * lax.axis_size("c") + lax.axis_index("c")
    half = lax.axis_index("c") if own_half else 1 - lax.axis_index("c")
    lane = lax.broadcasted_iota(jnp.int32, (128, 128), 1)
    inner_lane = jnp.bitwise_and(lane, LH - 1)
    group_lane = lane // LH
    flips = (1 - 2 * signs_ref[...]).astype(jnp.float32)
    strips = []
    for part in range(2):
        start = pl.multiple_of(half * count + chunk * 256 + part * 128, 128)
        picks = jnp.broadcast_to(picks_ref[:, pl.ds(start, 128)], (128, 128)).T
        owners = jnp.right_shift(picks, rows.bit_length() - 1)
        bits = jnp.bitwise_and(jnp.bitwise_and(picks, LH - 1), inner_lane)
        bits = parity(jnp.bitwise_xor(bits, parity(jnp.bitwise_and(owners, group_mine))))
        values = (1 - 2 * bits).astype(jnp.float32)
        group = jnp.right_shift(jnp.bitwise_and(picks, rows - 1), 5) - group_lane
        strips.append((values, group))
    tiles = []
    for tile in range(rows // 128):
        flip = flips[:, tile * 128 : tile * 128 + 128]
        tiles.append(
            jnp.concatenate(
                [jnp.where(group == 4 * tile, values * flip, 0.0).astype(jnp.bfloat16)
                 for values, group in strips],
                axis=0,
            )
        )
    return jnp.concatenate(tiles, axis=1)


def sketch_sent_kernel(
    picks_hbm, signs_hbm, panel_hbm, out_ref, picks_ref, signs_ref, panel_ref, chosen, sems
):
    copies = [
        pltpu.make_async_copy(source, target, sems.at[place])
        for place, (source, target) in enumerate(
            ((picks_hbm, picks_ref), (signs_hbm, signs_ref), (panel_hbm, panel_ref))
        )
    ]
    for copy in copies:
        copy.start()
    copies[0].wait()
    copies[1].wait()
    count = out_ref.shape[0]
    for chunk in range(count // 256):
        chosen[chunk * 256 : chunk * 256 + 256, :] = choice(
            False, count, picks_ref, signs_ref, chunk
        )
    copies[2].wait()
    for start in range(0, count, 256):
        out_ref[start : start + 256, :] = dot(chosen[start : start + 256, :], panel_ref[...])


def sketch_own_kernel(picks_ref, signs_ref, panel_ref, out_ref):
    count = out_ref.shape[0]
    for chunk in range(count // 256):
        out_ref[chunk * 256 : chunk * 256 + 256, :] = dot(
            choice(True, count, picks_ref, signs_ref, chunk), panel_ref[...]
        )


def sketch_sent(picks, signs, panel):
    count, (rows, columns) = picks.shape[1] // 2, panel.shape
    return pl.pallas_call(
        sketch_sent_kernel,
        out_shape=(
            jax.ShapeDtypeStruct((count, columns), jnp.float32),
            jax.ShapeDtypeStruct(picks.shape, picks.dtype),
            jax.ShapeDtypeStruct(signs.shape, signs.dtype),
            jax.ShapeDtypeStruct(panel.shape, panel.dtype),
        ),
        in_specs=[pl.BlockSpec(memory_space=pltpu.HBM)] * 3,
        out_specs=(VMEM,) * 4,
        scratch_shapes=[
            pltpu.VMEM((count, rows), jnp.bfloat16),
            pltpu.SemaphoreType.DMA((3,)),
        ],
        compiler_params=PARAMS,
        name="sketch_sent",
    )(picks, signs, panel)


def sketch_own(picks, signs, panel):
    return pl.pallas_call(
        sketch_own_kernel,
        out_shape=jax.ShapeDtypeStruct((picks.shape[1] // 2, panel.shape[1]), jnp.float32),
        in_specs=[VMEM] * 3,
        out_specs=VMEM,
        compiler_params=PARAMS,
        name="sketch_own",
    )(picks, signs, panel)


def pack_gram(matrix, kept_ref, sent_ref, precision):
    columns = matrix.shape[1]
    blocks = []
    for i in range(columns // GB):
        strip = dot(matrix[:, i * GB : i * GB + GB], matrix[:, i * GB :], 0, 0, precision)
        blocks += [strip[:, j * GB : j * GB + GB] for j in range(columns // GB - i)]
    first = lax.axis_index("c") == 0
    half = len(blocks) // 2
    for place in range(half):
        own = slice(place * GB, place * GB + GB)
        kept_ref[own, :] = jnp.where(first, blocks[place], blocks[place + half])
        sent_ref[own, :] = jnp.where(first, blocks[place + half], blocks[place])


def half_shape(columns):
    return jax.ShapeDtypeStruct((len(upper_blocks(columns)) // 2 * GB, GB), jnp.float32)


def sketch_gram_kernel(parts_ref, kept_ref, sent_ref):
    pack_gram(jnp.sum(parts_ref[...], axis=0), kept_ref, sent_ref, HIGHEST)


def sketch_gram(parts):
    columns = parts.shape[2]
    return pl.pallas_call(
        sketch_gram_kernel,
        out_shape=(half_shape(columns),) * 2,
        in_specs=[VMEM],
        out_specs=(VMEM, VMEM),
        compiler_params=PARAMS,
        name="sketch_gram",
    )(parts)


def times_inverse(rows_ref, inverse, buffer, out_ref, sems):
    rows, columns = rows_ref.shape
    half = columns // 2
    copies = []
    for place, start in enumerate(range(0, rows, 512)):
        own = pl.ds(start, 512)
        buffer[own, :half] = dot(
            rows_ref[own, :half], inverse[:half, :half], 1, 1
        ).astype(jnp.bfloat16)
        buffer[own, half:] = dot(rows_ref[own, :], inverse[half:, :], 1, 1).astype(jnp.bfloat16)
        copies.append(pltpu.make_async_copy(buffer.at[own, :], out_ref.at[own, :], sems.at[place]))
        copies[-1].start()
    return copies


def spread_row(tile, k):
    return jnp.broadcast_to(tile[k : k + 1, :], tile.shape)


def spread_lane(tile, c):
    return jnp.broadcast_to(tile[:, c : c + 1], tile.shape)


def factor_block(block):
    row = lax.broadcasted_iota(jnp.int32, (NB, NB), 0)
    column = lax.broadcasted_iota(jnp.int32, (NB, NB), 1)
    both = jnp.concatenate([block, (row == column).astype(jnp.float32)], axis=1)
    count = NB // 8
    work = [both[8 * u : 8 * u + 8, :] for u in range(count)]
    sub = lax.broadcasted_iota(jnp.int32, (8, 128), 0)
    done = []
    ahead = [spread_lane(work[0], c) for c in range(8)]
    for t in range(count):
        lanes = {u: [spread_lane(work[u], 8 * t + c) for c in range(8)] for u in range(t + 1, count)}
        lanes[t] = ahead
        if t + 1 < count:
            beside = [spread_lane(work[t], 8 * t + 8 + c) for c in range(8)]
            ahead = [spread_lane(work[t + 1], 8 * t + 8 + c) for c in range(8)]
        pivots = pivot = spread_row(lanes[t][0], 0)
        for k in range(8):
            inverse = 1.0 / pivot
            pivots = jnp.where(sub == k, pivot, pivots)
            across = {c: spread_row(lanes[t][c], k) for c in range(k + 1, 8)}
            if k < 7:
                pivot = spread_row(lanes[t][k + 1], k + 1) - (across[k + 1] * inverse) * across[k + 1]
            pivot_row = spread_row(work[t], k)
            ratio = jnp.where(sub > k, lanes[t][k], 0.0) * inverse
            for c in range(k + 1, 8):
                lanes[t][c] = lanes[t][c] - ratio * across[c]
            if t + 1 < count:
                next_ratio = lanes[t + 1][k] * inverse
                for c in range(8):
                    entry = spread_row(beside[c], k)
                    beside[c] = beside[c] - ratio * entry
                    ahead[c] = ahead[c] - next_ratio * entry
            if k < 7:
                work[t] = work[t] - ratio * pivot_row
            for u in range(t + 1, count):
                ratio = lanes[u][k] * inverse
                for c in range(k + 1, 8):
                    lanes[u][c] = lanes[u][c] - ratio * across[c]
                work[u] = work[u] - ratio * pivot_row
        done.append(work[t] * lax.rsqrt(pivots))
    return jnp.concatenate(done, axis=0)


def split(value):
    first = value.astype(jnp.bfloat16)
    left = value - first.astype(jnp.float32)
    second = left.astype(jnp.bfloat16)
    third = (left - second.astype(jnp.float32)).astype(jnp.bfloat16)
    return first, second, third


def left_terms(value, axis):
    first, second, third = split(value)
    return jnp.concatenate([first, first, second, second, first, third], axis=axis)


def right_terms(value, axis):
    first, second, third = split(value)
    return jnp.concatenate([first, second, first, second, third, first], axis=axis)


def factor_into(scale, own_ref, other_ref, factor_ref, inverse_ref, work, run=None):
    order = work.shape[0]
    first = lax.axis_index("c") == 0
    blocks = upper_blocks(order)
    half = len(blocks) // 2
    for place in range(half):
        rows = slice(place * GB, place * GB + GB)
        own, other = own_ref[rows, :] * scale, other_ref[rows, :] * scale
        for which, block in (
            (place, jnp.where(first, own, other)),
            (place + half, jnp.where(first, other, own)),
        ):
            i, j = blocks[which]
            work[i * GB : i * GB + GB, j * GB : j * GB + GB] = block
            if i != j:
                work[j * GB : j * GB + GB, i * GB : i * GB + GB] = block.T
    (run or eliminate)(factor_ref, inverse_ref, work)


def times(first, second, first_dim=1, second_dim=0):
    return dot(left_terms(first, first_dim), right_terms(second, second_dim), first_dim, second_dim)


def factor_pair(block):
    row = lax.broadcasted_iota(jnp.int32, (NB, NB), 0)
    column = lax.broadcasted_iota(jnp.int32, (NB, NB), 1)
    zero = jnp.zeros((NB, NB), jnp.float32)
    first = factor_block(block[:NB, :NB])
    first_factor = jnp.where(row <= column, first[:, :NB], 0.0)
    first_inverse = first[:, NB:]
    above = times(first_inverse, block[:NB, NB:])
    below = times(block[NB:, :NB], first_inverse, 1, 1)
    second = factor_block(block[NB:, NB:] - times(below, above))
    second_factor = jnp.where(row <= column, second[:, :NB], 0.0)
    second_inverse = second[:, NB:]
    corner = -times(second_inverse, times(below, first_inverse))
    factor = jnp.concatenate(
        [jnp.concatenate([first_factor, above], axis=1), jnp.concatenate([zero, second_factor], axis=1)],
        axis=0,
    )
    inverse = jnp.concatenate(
        [jnp.concatenate([first_inverse, zero], axis=1), jnp.concatenate([corner, second_inverse], axis=1)],
        axis=0,
    )
    return factor, inverse


def eliminate(factor_ref, inverse_ref, work):
    order = work.shape[0]
    size = 2 * NB
    row = lax.broadcasted_iota(jnp.int32, (size, size), 0)
    column = lax.broadcasted_iota(jnp.int32, (size, size), 1)
    wide = lax.broadcasted_iota(jnp.int32, (size, order), 1)

    def apply(start, diagonal, inverse):
        own, rest = slice(start, start + size), slice(start + size, order)
        if start + size < order:
            left = dot(right_terms(work[rest, own], 1), inverse, 1, 1)
        work[own, own] = (row == column).astype(jnp.float32)
        strip = dot(inverse, right_terms(work[own, :], 0))
        inverse_ref[own, :] = jnp.where(wide < start + size, strip, 0.0).astype(jnp.bfloat16)
        factor_ref[own, :] = jnp.where(wide >= start + size, strip, 0.0)
        factor_ref[own, own] = diagonal
        if start + size < order:
            work[rest, own] = jnp.zeros((order - start - size, size), jnp.float32)
            work[rest, :] = work[rest, :] - dot(left_terms(left, 1), right_terms(strip, 0))

    def step(place, carry):
        own = pl.ds(pl.multiple_of(place * size, size), size)
        diagonal, inverse = factor_pair(work[own, own])
        inverse = left_terms(inverse, 1)
        for start in range(0, order, size):
            pl.when(place * size == start)(functools.partial(apply, start, diagonal, inverse))
        return carry

    lax.fori_loop(0, order // size, step, 0)


def eliminate_whole(factor_ref, inverse_ref, work):
    order = work.shape[0]
    row = lax.broadcasted_iota(jnp.int32, (NB, NB), 0)
    column = lax.broadcasted_iota(jnp.int32, (NB, NB), 1)
    wide = lax.broadcasted_iota(jnp.int32, (NB, order), 1)
    for end in range(NB, order + 1, NB):
        own = slice(end - NB, end)
        rest = slice(end, order)
        both = factor_block(work[own, own])
        diagonal = jnp.where(row <= column, both[:, :NB], 0.0)
        inverse = left_terms(both[:, NB:], 1)
        if end < order:
            left = dot(right_terms(work[rest, own], 1), inverse, 1, 1)
        work[own, own] = (row == column).astype(jnp.float32)
        strip = dot(inverse, right_terms(work[own, :], 0))
        inverse_ref[own, :] = jnp.where(wide < end, strip, 0.0).astype(jnp.bfloat16)
        factor_ref[own, :] = jnp.where(wide >= end, strip, 0.0)
        factor_ref[own, own] = diagonal
        if end < order:
            work[rest, own] = jnp.zeros((order - end, NB), jnp.float32)
            work[rest, :] = work[rest, :] - dot(left_terms(left, 1), right_terms(strip, 0))


def whiten_kernel(
    scale, own_ref, other_ref, panel_ref, factor_ref, white_ref, kept_ref, sent_ref,
    work, inverse, buffer, sems,
):
    factor_into(scale, own_ref, other_ref, factor_ref, inverse, work)
    copies = times_inverse(panel_ref, inverse, buffer, white_ref, sems)
    pack_gram(buffer[...], kept_ref, sent_ref, None)
    for copy in copies:
        copy.wait()


def finish_kernel(
    scale, own_ref, other_ref, white_hbm, factor_ref, out_ref, work, inverse, buffer, sems, white_ref, arrived
):
    arrival = pltpu.make_async_copy(white_hbm.at[pl.ds(0, white_ref.shape[0]), :], white_ref, arrived)
    arrival.start()
    factor_into(scale, own_ref, other_ref, factor_ref, inverse, work, eliminate_whole)
    arrival.wait()
    for copy in times_inverse(white_ref, inverse, buffer, out_ref, sems):
        copy.wait()


HBM = pl.BlockSpec(memory_space=pltpu.HBM)
STRETCH = 16


def scratch(rows, order):
    return [
        pltpu.VMEM((order, order), jnp.float32),
        pltpu.VMEM((order, order), jnp.bfloat16),
        pltpu.VMEM((rows, order), jnp.bfloat16),
        pltpu.SemaphoreType.DMA((rows // 512,)),
    ]


def whiten(scale, own, other, panel):
    rows, order = panel.shape
    return pl.pallas_call(
        functools.partial(whiten_kernel, scale),
        out_shape=(
            jax.ShapeDtypeStruct((order, order), jnp.float32),
            jax.ShapeDtypeStruct((STRETCH * rows, order), jnp.bfloat16),
            half_shape(order),
            half_shape(order),
        ),
        in_specs=[VMEM] * 3,
        out_specs=(VMEM, HBM, VMEM, VMEM),
        scratch_shapes=scratch(rows, order),
        compiler_params=PARAMS,
        name="whiten",
    )(own, other, panel)


def finish(scale, own, other, whitened):
    rows, order = whitened.shape[0] // STRETCH, whitened.shape[1]
    return pl.pallas_call(
        functools.partial(finish_kernel, scale),
        out_shape=(
            jax.ShapeDtypeStruct((order, order), jnp.float32),
            jax.ShapeDtypeStruct((rows, order), jnp.bfloat16),
        ),
        in_specs=[VMEM, VMEM, HBM],
        out_specs=(VMEM, HBM),
        scratch_shapes=scratch(rows, order)
        + [pltpu.VMEM((rows, order), jnp.bfloat16), pltpu.SemaphoreType.DMA],
        compiler_params=PARAMS,
        name="finish",
    )(own, other, whitened)


def sum_all(kept, sent):
    swap = [(0, 1), (1, 0)]
    kept = kept + lax.ppermute(sent, "c", swap)
    count = lax.axis_size(CHIPS)
    parts = kept.reshape(count, kept.shape[0] // count // 2, 2, GB)
    parts = lax.all_to_all(parts, CHIPS, 0, 0, tiled=True)
    total = jnp.sum(parts, axis=0, keepdims=True)
    parts = jnp.broadcast_to(total, parts.shape)
    own = lax.all_to_all(parts, CHIPS, 0, 0, tiled=True).reshape(kept.shape)
    return own, lax.ppermute(own, "c", swap)


def on_device(panel, signs, sample_rows):
    n_had = lax.axis_size("z") * lax.axis_size("c")
    n_blk = lax.axis_size("x") * lax.axis_size("y")
    rows_dev, columns = panel.shape
    sketch_count = sample_rows.shape[1]
    signs = signs.reshape(1, rows_dev)
    sent, picks_near, signs_near, panel_near = sketch_sent(sample_rows, signs, panel)
    other = lax.ppermute(sent, "c", [(0, 1), (1, 0)])
    mine = sketch_own(picks_near, signs_near, panel_near) + other
    chips = lax.axis_size(CHIPS)
    mine = mine.reshape(chips, sketch_count // 2 // chips, columns)
    parts = lax.all_to_all(mine, CHIPS, 0, 0, tiled=True)
    own, other = sum_all(*sketch_gram(parts))
    r_sketch, whitened, kept, sent = whiten(
        1.0 / (n_had * LH * sketch_count * n_blk), own, other, panel
    )
    own, other = sum_all(kept, sent)
    r_gram, q_panel = finish(1.0 / (rows_dev * n_had * n_blk), own, other, whitened)
    return (q_panel, r_sketch, r_gram)


def solution(mesh):
    devices = mesh.devices.reshape(4, 2, 4, 4)
    split = Mesh(devices, AXES)
    placed = (P(AXES, None), P(AXES), P(("x", "y"), None))
    return jax.shard_map(
        on_device,
        mesh=split,
        in_specs=placed,
        out_specs=(P(AXES, None), P(), P()),
        check_vma=False,
    )
```
